32 devices in a mesh: dom: 8 (over y, x, core), cls: 4 (over z).
Axes of the slice: x: 2, y: 2, z: 4, core: 2. Of those that a mesh axis runs over, the one named last changes fastest.
Arguments:
- images: bfloat16 [1024, 64, 256], P('dom'), may hold values from -48 to 48
- class_refs: bfloat16 [64, 64, 256], P('cls', 'dom'), may hold values from -1 to 1
- ctf_table: float32 [64, 64], replicated, may hold values from 0.1 to 1
- ctf_group: int32 [1024], P('dom'), may hold values from 0 to 63
- prior_angle: int32 [1024], P('dom'), may hold values from 0 to 255
- precision: float32 [1024], P('dom'), may hold values from 0.25 to 4
Outputs:
- new_refs: float32 [64, 64, 256], P('cls', 'dom')
- log_evidence: float32 [1024], P('dom')
The draws below stay inside these ranges and needn't reach their ends.
All inputs are finite; a program needn't handle non-finite values.
Results may differ from the reference program's by a relative error of at most 0.007.
Values may be sent and summed in bfloat16 or wider, within the bound.
A program may use at most 128 MiB of HBM per device.

```python
import math
import jax
import jax.numpy as jnp
from jax import lax

R = 64
A = 256
K = 64
G = 64
PART_DEV = 128
PART = 1024
N_DOM = 8


def common_refs(key):
    base = jax.random.normal(jax.random.fold_in(key, 11), (K, R, A), jnp.float32)
    return jnp.clip(base, -6.0, 6.0) / math.sqrt(R * A)


def draw_class_refs(key, part):
    return common_refs(key).astype(jnp.bfloat16)


def draw_images(key, part):
    refs = common_refs(key)
    noise = jnp.clip(jax.random.normal(jax.random.fold_in(key, 12), (PART, R, A), jnp.float32), -6.0, 6.0)
    pairing = jax.random.permutation(jax.random.fold_in(key, 14), N_DOM)
    owner = jnp.arange(PART, dtype=jnp.int32) // PART_DEV
    cycle_block = jnp.arange(R, dtype=jnp.int32) // (R // N_DOM)
    boost = jnp.where(pairing[owner][:, None] == cycle_block[None, :], 4.0, 1.0)
    chosen = jax.random.randint(jax.random.fold_in(key, 13), (PART,), 0, K)
    turn = jax.random.randint(jax.random.fold_in(key, 15), (PART,), 0, A)
    strength = jax.random.uniform(jax.random.fold_in(key, 16), (PART,), jnp.float32, 40.0, 240.0)
    aligned = jnp.arange(PART, dtype=jnp.int32) % 4 == 0
    strength = jnp.where(aligned, strength, 0.0)
    index = (jnp.arange(A, dtype=jnp.int32)[None, :] - turn[:, None]) % A
    picked = refs[chosen]
    rotated = jnp.take_along_axis(picked, jnp.broadcast_to(index[:, None, :], (PART, R, A)), axis=2)
    values = noise * boost[:, :, None] + strength[:, None, None] * rotated
    return jnp.clip(values, -48.0, 48.0).astype(jnp.bfloat16)


def with_ends(values, stream_key, smallest, largest):
    place = [jax.random.randint(jax.random.fold_in(stream_key, axis), (), 0, length) for axis, length in enumerate(values.shape)]
    longest = values.shape.index(max(values.shape))
    beside = place[:longest] + [(place[longest] + 1) % values.shape[longest]] + place[longest + 1:]
    return values.at[tuple(place)].set(smallest).at[tuple(beside)].set(largest)


def level_of(own_key, shape, shards, low, high):
    def one(position, shards_of):
        heights = jax.random.uniform(jax.random.fold_in(jax.random.fold_in(own_key, 6), position), (shards_of,), jnp.float32, low / len(shards), high / len(shards))
        return jnp.repeat(jnp.exp(heights), shape[position] // shards_of).reshape((-1,) + (1,) * (len(shape) - position - 1))

    factor_of = one(*shards[0])
    for cut in shards[1:]:
        factor_of = factor_of * one(*cut)
    return factor_of


def setup_inputs(seed: int = 0) -> dict:
    key_list = jax.random.split(jax.random.key(seed), 7)
    return {
        "images": draw_images(jax.random.fold_in(key_list[6], 71), 0),
        "class_refs": draw_class_refs(jax.random.fold_in(key_list[6], 71), 0),
        "ctf_table": jnp.clip(jax.random.uniform(key_list[2], (G, R), jnp.float32, 0.1, 1.0), 0.1, 1.0),
        "ctf_group": with_ends(jax.random.randint(key_list[3], (PART,), 0, G), jax.random.fold_in(key_list[3], 1), 0, G - 1).astype(jnp.int32),
        "prior_angle": with_ends(jax.random.randint(key_list[4], (PART,), 0, A), jax.random.fold_in(key_list[4], 1), 0, A - 1).astype(jnp.int32),
        "precision": jnp.clip(jnp.exp(math.log(4.0) - 2.7725887 * jax.random.uniform(key_list[5], (PART,), jnp.float32) ** level_of(key_list[5], (PART,), ((0, 8),), -0.2, 0.2)), 0.25, 4.0),
    }


prior_strength = 2.0
ridge = 1.0
highest = lax.Precision.HIGHEST


def angle_table(angle_count, mode_count):
    angles = jnp.arange(angle_count, dtype=jnp.int32)
    freqs = jnp.arange(mode_count, dtype=jnp.int32)
    product = (angles[:, None] * freqs[None, :]) % angle_count
    phase = product.astype(jnp.float32) * (2.0 * math.pi / angle_count)
    return jnp.concatenate([jnp.cos(phase), jnp.sin(phase)], axis=1)


def split_table(forward):
    upper = forward.astype(jnp.bfloat16)
    lower = (forward - upper.astype(jnp.float32)).astype(jnp.bfloat16)
    return (upper, lower)


def mode_weights(angle_count, mode_count):
    freqs = jnp.arange(mode_count, dtype=jnp.int32)
    single = jnp.where(freqs == 0, 1.0, 2.0).astype(jnp.float32) / angle_count
    return jnp.concatenate([single, single])


def synthesis_table(angle_count, mode_count):
    return jnp.transpose(angle_table(angle_count, mode_count)) * mode_weights(angle_count, mode_count)[:, None]


def spectrum(values, forward_pair):
    upper, lower = forward_pair
    flat = values.reshape(-1, values.shape[-1])
    result = jnp.dot(flat, upper, preferred_element_type=jnp.float32)
    result = result + jnp.dot(flat, lower, preferred_element_type=jnp.float32)
    return result.reshape(values.shape[:-1] + (upper.shape[1],))


def prior_term(prior_angle, angle_count):
    rotations = jnp.arange(angle_count, dtype=jnp.int32)
    offsets = (rotations[None, :] - prior_angle[:, None]) % angle_count
    return prior_strength * jnp.cos(offsets.astype(jnp.float32) * (2.0 * math.pi / angle_count))


def pair_refs(spec_four):
    cos_part = spec_four[:, :, 0]
    sin_part = spec_four[:, :, 1]
    first_pair = jnp.stack([cos_part, sin_part], axis=2)
    second_pair = jnp.stack([-sin_part, cos_part], axis=2)
    return jnp.stack([first_pair, second_pair], axis=1)


def pair_weights(spec_four):
    cos_part = spec_four[:, :, 0]
    sin_part = spec_four[:, :, 1]
    first_pair = jnp.stack([cos_part, sin_part], axis=2)
    second_pair = jnp.stack([-sin_part, cos_part], axis=2)
    return jnp.stack([first_pair, second_pair], axis=2)


def reference(images, class_refs, ctf_table, ctf_group, prior_angle, precision):
    mode_count = A // 2
    forward = angle_table(A, mode_count)
    forward_pair = split_table(forward)
    synthesis = synthesis_table(A, mode_count)
    ref_spectra = spectrum(class_refs, forward_pair).astype(jnp.bfloat16)
    ref_float = ref_spectra.astype(jnp.float32)
    cycle_energy = jnp.sum(ref_float * ref_float * mode_weights(A, mode_count), axis=2)
    ref_pairs = pair_refs(ref_float.reshape(K, R, 2, mode_count))

    def block_step(carry, inputs):
        sums_acc, totals_acc = carry
        image_block, group_block, angle_block, precision_block = inputs
        block_rows = image_block.shape[0]
        ctf_rows = ctf_table[group_block]
        particle_spectra = (ctf_rows[:, :, None] * spectrum(image_block, forward_pair)).astype(jnp.bfloat16)
        particle_four = particle_spectra.astype(jnp.float32).reshape(block_rows, R, 2, mode_count)
        cross = jnp.einsum('prhm,kjrhm->pkjm', particle_four, ref_pairs, precision=highest)
        correlation = jnp.dot(cross.reshape(-1, A), synthesis, precision=highest, preferred_element_type=jnp.float32)
        correlation = correlation.reshape(block_rows, K, A)
        ctf_square = ctf_rows * ctf_rows
        energy = jnp.dot(ctf_square, jnp.transpose(cycle_energy), precision=highest, preferred_element_type=jnp.float32)
        score = precision_block[:, None, None] * (correlation - 0.5 * energy[:, :, None])
        score = score + prior_term(angle_block, A)[:, None, :]
        row_top = jnp.max(score, axis=(1, 2))
        sum_exp = jnp.sum(jnp.exp(score - row_top[:, None, None]), axis=(1, 2))
        evidence = row_top + jnp.log(sum_exp)
        weights = jnp.exp(score - evidence[:, None, None]).astype(jnp.bfloat16)
        weight_spectra = spectrum(weights, forward_pair).astype(jnp.bfloat16)
        mass = jnp.sum(weights.astype(jnp.float32), axis=2)
        weight_pairs = pair_weights(weight_spectra.astype(jnp.float32).reshape(block_rows, K, 2, mode_count))
        block_sums = jnp.einsum('pkjhm,prhm->rkjm', weight_pairs, particle_four, precision=highest)
        block_totals = jnp.dot(jnp.transpose(mass), ctf_square, precision=highest, preferred_element_type=jnp.float32)
        return (sums_acc + block_sums.reshape(R, K, A), totals_acc + block_totals), evidence

    inputs = (images.reshape(N_DOM, PART_DEV, R, A), ctf_group.reshape(N_DOM, PART_DEV),
              prior_angle.reshape(N_DOM, PART_DEV), precision.reshape(N_DOM, PART_DEV))
    initial = (jnp.zeros((R, K, A), jnp.float32), jnp.zeros((K, R), jnp.float32))
    (class_sums, totals), evidence = lax.scan(block_step, initial, inputs)
    new_spectra = class_sums / (jnp.transpose(totals) + ridge)[:, :, None]
    new_refs = jnp.dot(new_spectra.reshape(-1, A), synthesis, precision=highest, preferred_element_type=jnp.float32)
    new_refs = jnp.transpose(new_refs.reshape(R, K, A), (1, 0, 2))
    return new_refs, evidence.reshape(PART)
```

```python
import functools
import math

import jax
import jax.numpy as jnp
import ml_dtypes
import numpy as np
from jax import lax
from jax.experimental import pallas as pl
from jax.experimental.pallas import tpu as pltpu
from jax.sharding import PartitionSpec as P

prior_strength = 2.0
ridge = 1.0
highest = lax.Precision.HIGHEST


def angle_table(angle_count, mode_count):
    angles = jnp.arange(angle_count, dtype=jnp.int32)
    freqs = jnp.arange(mode_count, dtype=jnp.int32)
    product = angles[:, None] * freqs[None, :] % angle_count
    phase = product.astype(jnp.float32) * (2.0 * math.pi / angle_count)
    return jnp.concatenate([jnp.cos(phase), jnp.sin(phase)], axis=1)


def split_table(forward):
    upper = forward.astype(jnp.bfloat16)
    lower = (forward - upper.astype(jnp.float32)).astype(jnp.bfloat16)
    return (upper, lower)


def mode_weights(angle_count, mode_count):
    freqs = jnp.arange(mode_count, dtype=jnp.int32)
    single = jnp.where(freqs == 0, 1.0, 2.0).astype(jnp.float32) / angle_count
    return jnp.concatenate([single, single])


def synthesis_table(angle_count, mode_count):
    return (
        jnp.transpose(angle_table(angle_count, mode_count))
        * mode_weights(angle_count, mode_count)[:, None]
    )


def spectrum(values, forward_pair):
    upper, lower = forward_pair
    flat = values.reshape(-1, values.shape[-1])
    result = jnp.dot(flat, upper, preferred_element_type=jnp.float32)
    result = result + jnp.dot(flat, lower, preferred_element_type=jnp.float32)
    return result.reshape(values.shape[:-1] + (upper.shape[1],))


def weighted_spectrum(images, ctf_rows, forward_pair):
    return (ctf_rows[:, :, None] * spectrum(images, forward_pair)).astype(jnp.bfloat16)


def prior_term(prior_angle, angle_count):
    rotations = jnp.arange(angle_count, dtype=jnp.int32)
    offsets = (rotations[None, :] - prior_angle[:, None]) % angle_count
    return prior_strength * jnp.cos(offsets.astype(jnp.float32) * (2.0 * math.pi / angle_count))


def pair_refs(spec_four):
    cos_part = spec_four[:, :, 0]
    sin_part = spec_four[:, :, 1]
    first_pair = jnp.stack([cos_part, sin_part], axis=2)
    second_pair = jnp.stack([-sin_part, cos_part], axis=2)
    return jnp.stack([first_pair, second_pair], axis=1)


def pair_weights(spec_four):
    cos_part = spec_four[:, :, 0]
    sin_part = spec_four[:, :, 1]
    first_pair = jnp.stack([cos_part, sin_part], axis=2)
    second_pair = jnp.stack([-sin_part, cos_part], axis=2)
    return jnp.stack([first_pair, second_pair], axis=2)


def local(images, class_refs, ctf_table, ctf_group, prior_angle, precision):
    particle_count, cycle_count, angle_count = images.shape
    mode_count = angle_count // 2
    class_count = class_refs.shape[0]
    forward = angle_table(angle_count, mode_count)
    forward_pair = split_table(forward)
    synthesis = synthesis_table(angle_count, mode_count)
    ref_local = spectrum(class_refs, forward_pair).astype(jnp.bfloat16)
    ref_spectra = lax.all_gather(ref_local, "dom", axis=1, tiled=True)
    group_ids = jnp.arange(ctf_table.shape[0], dtype=jnp.int32)
    one_hot = (ctf_group[:, None] == group_ids[None, :]).astype(jnp.float32)
    ctf_rows = jnp.dot(one_hot, ctf_table, precision=highest, preferred_element_type=jnp.float32)
    ctf_square = ctf_rows * ctf_rows
    particle_spectra = weighted_spectrum(images, ctf_rows, forward_pair)
    ref_float = ref_spectra.astype(jnp.float32)
    cycle_energy = jnp.sum(ref_float * ref_float * mode_weights(angle_count, mode_count), axis=2)
    energy = jnp.dot(
        ctf_square,
        jnp.transpose(cycle_energy),
        precision=highest,
        preferred_element_type=jnp.float32,
    )
    particle_four = particle_spectra.reshape(particle_count, cycle_count, 2, mode_count)
    ref_pairs = pair_refs(ref_spectra.reshape(class_count, cycle_count, 2, mode_count))
    cross = jnp.einsum(
        "prhm,kjrhm->pkjm", particle_four, ref_pairs, preferred_element_type=jnp.float32
    )
    correlation = jnp.dot(
        cross.reshape(-1, angle_count),
        synthesis,
        precision=highest,
        preferred_element_type=jnp.float32,
    )
    correlation = correlation.reshape(particle_count, class_count, angle_count)
    score = precision[:, None, None] * (correlation - 0.5 * energy[:, :, None])
    score = score + prior_term(prior_angle, angle_count)[:, None, :]
    row_top = jnp.max(score, axis=(1, 2))
    peak = lax.pmax(row_top, "cls")
    local_sum = jnp.sum(jnp.exp(score - peak[:, None, None]), axis=(1, 2))
    sum_exp = lax.psum(local_sum, "cls")
    log_evidence = peak + jnp.log(sum_exp)
    weights = jnp.exp(score - log_evidence[:, None, None]).astype(jnp.bfloat16)
    weight_spectra = spectrum(weights, forward_pair).astype(jnp.bfloat16)
    mass = jnp.sum(weights.astype(jnp.float32), axis=2)
    weight_pairs = pair_weights(weight_spectra.reshape(particle_count, class_count, 2, mode_count))
    class_sums = jnp.einsum(
        "pkjhm,prhm->rkjm", weight_pairs, particle_four, preferred_element_type=jnp.float32
    )
    class_sums = class_sums.reshape(cycle_count, class_count, angle_count)
    totals = jnp.dot(
        jnp.transpose(ctf_square), mass, precision=highest, preferred_element_type=jnp.float32
    )
    whole_sums, whole_totals = lax.psum((class_sums, totals), "dom")
    cycle_share = cycle_count // lax.axis_size("dom")
    cycle_start = lax.axis_index("dom") * cycle_share
    cycle_sums = lax.dynamic_slice_in_dim(whole_sums, cycle_start, cycle_share, 0)
    cycle_totals = lax.dynamic_slice_in_dim(whole_totals, cycle_start, cycle_share, 0)
    new_spectra = cycle_sums / (cycle_totals + ridge)[:, :, None]
    new_refs = jnp.dot(
        new_spectra.reshape(-1, angle_count),
        synthesis,
        precision=highest,
        preferred_element_type=jnp.float32,
    )
    new_refs = jnp.transpose(
        new_refs.reshape(cycle_sums.shape[0], class_count, angle_count), (1, 0, 2)
    )
    return (new_refs, log_evidence)


def nt(left, right, precision=None):
    return lax.dot_general(
        left,
        right,
        (((1,), (1,)), ((), ())),
        precision=precision,
        preferred_element_type=jnp.float32,
    )


def nn(left, right, precision=None):
    return jnp.dot(left, right, precision=precision, preferred_element_type=jnp.float32)


def halves(value):
    upper = value.astype(jnp.bfloat16)
    lower = (value - upper.astype(jnp.float32)).astype(jnp.bfloat16)
    return upper, lower


def rounded(value):
    return value.astype(jnp.bfloat16).astype(jnp.float32)


def host_tables(angle_count, mode_count):
    product = np.outer(np.arange(angle_count), np.arange(mode_count)) % angle_count
    phase = product * (2.0 * math.pi / angle_count)
    forward = np.concatenate([np.cos(phase), np.sin(phase)], axis=1).astype(np.float32)
    single = np.where(np.arange(mode_count) == 0, 1.0, 2.0) / angle_count
    scale = np.concatenate([single, single]).astype(np.float32)
    inverse = forward * scale[None, :]

    def split(table):
        upper = table.astype(ml_dtypes.bfloat16)
        lower = (table - upper.astype(np.float32)).astype(ml_dtypes.bfloat16)
        return upper, lower

    return split(np.ascontiguousarray(forward.T)) + split(inverse)


def whole_kernel(
    dom_size, cls_size, img, refs, table, group, angle, prec, fwd_hi, fwd_lo, inv_hi, inv_lo,
    out_new, out_log, ref_slots, ref_rows, ctf, spec, ref_spec, cross, score, sums, send, recv,
    tot_send, tot_recv, stat_send, stat_recv, ref_sems, stat_sems, sum_sems, tot_sems,
):
    mesh_ids = pl.DeviceIdType.MESH
    dom, cls = lax.axis_index("dom"), lax.axis_index("cls")
    parts, cycles, angles = img.shape
    modes = angles // 2
    share = cycles // dom_size
    classes = refs.shape[0] // share
    barrier = pltpu.get_barrier_semaphore()
    for step in range(1, dom_size):
        pl.semaphore_signal(barrier, inc=1, device_id={"dom": lax.rem(dom + step, dom_size)}, device_id_type=mesh_ids)
    for step in range(1, cls_size):
        pl.semaphore_signal(barrier, inc=1, device_id={"cls": lax.rem(cls + step, cls_size)}, device_id_type=mesh_ids)
    pl.semaphore_wait(barrier, dom_size + cls_size - 2)

    def remote(source, target, sems, axis, place, size, step):
        return pltpu.make_async_remote_copy(
            src_ref=source,
            dst_ref=target,
            send_sem=sems.at[0, step],
            recv_sem=sems.at[1, step],
            device_id={axis: lax.rem(place + step, size)},
            device_id_type=mesh_ids,
        )

    ref_copies = [
        remote(refs, ref_slots.at[step], ref_sems, "dom", dom, dom_size, step)
        for step in range(1, dom_size)
    ]
    for copy in ref_copies:
        copy.start()

    lanes = lax.broadcasted_iota(jnp.int32, (modes, modes), 1)
    low = lanes < cycles
    groups = lax.broadcasted_iota(jnp.int32, (parts, table.shape[0]), 1)
    one_hot = (groups == group[...]).astype(jnp.float32)
    ctf[...] = nn(one_hot, table[...], highest)

    def transform(block):
        result = nt(fwd_hi[...], block) + nt(fwd_lo[...], block)
        found = []
        for pair in range(2):
            top = result[:modes, pair * modes : (pair + 1) * modes]
            bottom = result[modes:, pair * modes : (pair + 1) * modes]
            found.append(jnp.where(low, top, pltpu.roll(bottom, cycles, 1)))
            found.append(jnp.where(low, pltpu.roll(top, cycles, 1), bottom))
        return found

    def image_step(step, carry):
        first = step * 4
        block = img[pl.ds(first, 4)].reshape(4 * cycles, angles)
        for offset, value in enumerate(transform(block)):
            row = ctf[pl.ds(first + offset, 1), :]
            spec[pl.ds(first + offset, modes, stride=parts), :] = value * row
        return carry

    lax.fori_loop(0, parts // 4, image_step, 0, unroll=2)

    for copy in ref_copies:
        copy.wait()
    for step in range(dom_size):
        source = refs[...] if step == 0 else ref_slots[step]
        source = source.astype(jnp.float32).reshape(classes, share, angles)
        owner = lax.rem(dom - step + dom_size, dom_size)
        ref_rows[:, pl.ds(pl.multiple_of(owner * share, share), share), :] = source
    rows = lax.broadcasted_iota(jnp.int32, (modes, modes), 0)
    weight = jnp.where(rows == 0, 1.0, 2.0) * (1.0 / angles)
    sign = jnp.where(lax.broadcasted_iota(jnp.int32, (classes, modes), 1) < cycles, 1.0, -1.0)
    energies = []
    for step in range(classes // 4):
        block = ref_rows[step * 4 : step * 4 + 4].reshape(4 * cycles, angles).astype(jnp.bfloat16)
        for offset, value in enumerate(transform(block)):
            index = step * 4 + offset
            value = rounded(value)
            energies.append(jnp.sum(value * value * weight, axis=0, keepdims=True))
            ref_spec[pl.ds(index, modes, stride=2 * classes), :] = value
            turned = pltpu.roll(value, cycles, 1)
            ref_spec[pl.ds(classes + index, modes, stride=2 * classes), :] = jnp.where(low, -turned, turned)
    ctf_square = ctf[...] * ctf[...]
    energy = nt(jnp.concatenate(energies, axis=0), ctf_square, highest)

    def cross_step(mode, carry):
        particles = spec[pl.ds(pl.multiple_of(mode * parts, parts), parts), :].astype(jnp.bfloat16)
        others = ref_spec[pl.ds(pl.multiple_of(mode * 2 * classes, 2 * classes), 2 * classes), :]
        cross[pl.ds(mode, 2 * classes, stride=modes), :] = nt(others.astype(jnp.bfloat16), particles)
        return carry

    lax.fori_loop(0, modes, cross_step, 0, unroll=8)

    turns = lax.broadcasted_iota(jnp.int32, (angles, parts), 0)
    offsets = (turns - angle[...] + angles) % angles
    prior = prior_strength * jnp.cos(offsets.astype(jnp.float32) * (2.0 * math.pi / angles))
    scale = prec[...]
    peak = None
    for index in range(classes):
        both = jnp.concatenate(
            [cross[index * modes : (index + 1) * modes, :],
             cross[(classes + index) * modes : (classes + index + 1) * modes, :]], axis=0)
        upper, lower = halves(both)
        found = nn(inv_hi[...], upper) + (nn(inv_hi[...], lower) + nn(inv_lo[...], upper))
        found = scale * (found - 0.5 * energy[index : index + 1, :]) + prior
        score[index] = found
        top = jnp.max(found, axis=0, keepdims=True)
        peak = top if peak is None else jnp.maximum(peak, top)
    total = jnp.zeros((1, parts), jnp.float32)
    for index in range(classes):
        total = total + jnp.sum(jnp.exp(score[index] - peak), axis=0, keepdims=True)
    stat_send[...] = jnp.concatenate([peak] * 4 + [total] * 4, axis=0)
    stat_copies = [
        remote(stat_send, stat_recv.at[step], stat_sems, "cls", cls, cls_size, step)
        for step in range(1, cls_size)
    ]
    for copy in stat_copies:
        copy.start()
    for copy in stat_copies:
        copy.wait()
    pairs = [(peak, total)]
    for step in range(1, cls_size):
        pairs.append((stat_recv[step, 0:1, :], stat_recv[step, 4:5, :]))
    best = peak
    for other, _ in pairs[1:]:
        best = jnp.maximum(best, other)
    whole = jnp.zeros((1, parts), jnp.float32)
    for other, part in pairs:
        whole = whole + part * jnp.exp(other - best)
    log_evidence = best + jnp.log(whole)
    out_log[...] = log_evidence

    masses = []
    for index in range(classes):
        weights = jnp.exp(score[index] - log_evidence).astype(jnp.bfloat16)
        masses.append(jnp.sum(weights.astype(jnp.float32), axis=0, keepdims=True))
        found = nn(fwd_hi[...], weights) + nn(fwd_lo[...], weights)
        cross[index * modes : (index + 1) * modes, :] = found[:modes]
        cross[(classes + index) * modes : (classes + index + 1) * modes, :] = found[modes:]
    tot_send[...] = nn(jnp.concatenate(masses, axis=0), ctf_square, highest)
    tot_copies = [
        remote(tot_send, tot_recv.at[step], tot_sems, "dom", dom, dom_size, step)
        for step in range(1, dom_size)
    ]
    for copy in tot_copies:
        copy.start()

    def sum_step(mode, carry):
        particles = spec[pl.ds(pl.multiple_of(mode * parts, parts), parts), :].astype(jnp.bfloat16)
        weights = cross[pl.ds(mode, 2 * classes, stride=modes), :].astype(jnp.bfloat16)
        found = nn(weights, particles)
        found = found[:classes] + sign * pltpu.roll(found[classes:], cycles, 1)
        sums[pl.ds(mode, classes, stride=modes), :] = found
        return carry

    lax.fori_loop(0, modes, sum_step, 0, unroll=8)

    for index in range(classes):
        turned = jnp.transpose(sums[index * modes : (index + 1) * modes, :])
        for part in range(dom_size):
            piece = jnp.concatenate(
                [turned[part * share : (part + 1) * share],
                 turned[cycles + part * share : cycles + (part + 1) * share]], axis=0)
            send[part, index * 2 * share : (index + 1) * 2 * share, :] = piece.astype(jnp.bfloat16)
    sum_copies = [
        remote(send.at[lax.rem(dom + step, dom_size)], recv.at[step], sum_sems, "dom", dom, dom_size, step)
        for step in range(1, dom_size)
    ]
    for copy in sum_copies:
        copy.start()
    for copy in tot_copies:
        copy.wait()
    totals = tot_send[...]
    for step in range(1, dom_size):
        totals = totals + tot_recv[step]
    columns = lax.broadcasted_iota(jnp.int32, (1, share, modes), 2)
    wanted = lax.broadcasted_iota(jnp.int32, (1, share, modes), 1) + dom * share
    picked = jnp.where(columns == wanted, totals[:, None, :], 0.0)
    divisor = jnp.sum(picked, axis=2, keepdims=True).reshape(classes * share, 1) + ridge
    for copy in sum_copies:
        copy.wait()
    gathered = send[dom].astype(jnp.float32)
    for step in range(1, dom_size):
        gathered = gathered + recv[step].astype(jnp.float32)
    gathered = gathered.reshape(classes, 2, share, modes)
    result = jnp.zeros((classes * share, angles), jnp.float32)
    for half in range(2):
        upper, lower = halves(gathered[:, half].reshape(classes * share, modes))
        hi = inv_hi[:, half * modes : (half + 1) * modes]
        lo = inv_lo[:, half * modes : (half + 1) * modes]
        result = result + nt(upper, hi) + (nt(lower, hi) + nt(upper, lo))
    out_new[...] = result / divisor


def fused(images, class_refs, ctf_table, ctf_group, prior_angle, precision):
    dom_size, cls_size = lax.axis_size("dom"), lax.axis_size("cls")
    parts, cycles, angles = images.shape
    modes = angles // 2
    classes, share, _ = class_refs.shape
    tables = host_tables(angles, modes)
    f32, bf16 = jnp.float32, jnp.bfloat16
    vmem = pl.BlockSpec(memory_space=pltpu.VMEM)
    new_refs, log_evidence = pl.pallas_call(
        functools.partial(whole_kernel, dom_size, cls_size),
        out_shape=(
            jax.ShapeDtypeStruct((classes * share, angles), f32),
            jax.ShapeDtypeStruct((1, parts), f32),
        ),
        in_specs=[vmem] * 10,
        out_specs=(vmem, vmem),
        scratch_shapes=[
            pltpu.VMEM((dom_size, classes * share, angles), bf16),
            pltpu.VMEM((classes, cycles, angles), f32),
            pltpu.VMEM((parts, modes), f32),
            pltpu.VMEM((modes * parts, modes), f32),
            pltpu.VMEM((modes * 2 * classes, modes), f32),
            pltpu.VMEM((2 * classes * modes, parts), f32),
            pltpu.VMEM((classes, angles, parts), f32),
            pltpu.VMEM((classes * modes, modes), f32),
            pltpu.VMEM((dom_size, classes * 2 * share, modes), bf16),
            pltpu.VMEM((dom_size, classes * 2 * share, modes), bf16),
            pltpu.VMEM((classes, modes), f32),
            pltpu.VMEM((dom_size, classes, modes), f32),
            pltpu.VMEM((8, parts), f32),
            pltpu.VMEM((cls_size, 8, parts), f32),
            pltpu.SemaphoreType.DMA((2, dom_size)),
            pltpu.SemaphoreType.DMA((2, cls_size)),
            pltpu.SemaphoreType.DMA((2, dom_size)),
            pltpu.SemaphoreType.DMA((2, dom_size)),
        ],
        compiler_params=pltpu.CompilerParams(
            collective_id=0, has_side_effects=True, vmem_limit_bytes=52 * 1024 * 1024
        ),
    )(
        images,
        class_refs.reshape(classes * share, angles),
        jnp.concatenate([ctf_table, ctf_table], axis=1),
        ctf_group[:, None],
        prior_angle[None, :],
        precision[None, :],
        *[jnp.asarray(table) for table in tables],
    )
    return new_refs.reshape(classes, share, angles), log_evidence.reshape(parts)


def pick(images, class_refs, *rest):
    parts, cycles, angles = images.shape
    classes, share, _ = class_refs.shape
    fits = angles == 256 and cycles == 64 and parts == 128 and share % 8 == 0 and classes % 16 == 0
    return (fused if fits else local)(images, class_refs, *rest)


def solution(mesh):
    in_specs = (P("dom", None, None), P("cls", "dom", None), P(), P("dom"), P("dom"), P("dom"))
    out_specs = (P("cls", "dom", None), P("dom"))
    return jax.shard_map(pick, mesh=mesh, in_specs=in_specs, out_specs=out_specs, check_vma=False)
```

```python
import functools
import math

import jax
import jax.numpy as jnp
import ml_dtypes
import numpy as np
from jax import lax
from jax.experimental import pallas as pl
from jax.experimental.pallas import tpu as pltpu
from jax.sharding import PartitionSpec as P

prior_strength = 2.0
ridge = 1.0
highest = lax.Precision.HIGHEST


def angle_table(angle_count, mode_count):
    angles = jnp.arange(angle_count, dtype=jnp.int32)
    freqs = jnp.arange(mode_count, dtype=jnp.int32)
    product = angles[:, None] * freqs[None, :] % angle_count
    phase = product.astype(jnp.float32) * (2.0 * math.pi / angle_count)
    return jnp.concatenate([jnp.cos(phase), jnp.sin(phase)], axis=1)


def split_table(forward):
    upper = forward.astype(jnp.bfloat16)
    lower = (forward - upper.astype(jnp.float32)).astype(jnp.bfloat16)
    return (upper, lower)


def mode_weights(angle_count, mode_count):
    freqs = jnp.arange(mode_count, dtype=jnp.int32)
    single = jnp.where(freqs == 0, 1.0, 2.0).astype(jnp.float32) / angle_count
    return jnp.concatenate([single, single])


def synthesis_table(angle_count, mode_count):
    return (
        jnp.transpose(angle_table(angle_count, mode_count))
        * mode_weights(angle_count, mode_count)[:, None]
    )


def spectrum(values, forward_pair):
    upper, lower = forward_pair
    flat = values.reshape(-1, values.shape[-1])
    result = jnp.dot(flat, upper, preferred_element_type=jnp.float32)
    result = result + jnp.dot(flat, lower, preferred_element_type=jnp.float32)
    return result.reshape(values.shape[:-1] + (upper.shape[1],))


def weighted_spectrum(images, ctf_rows, forward_pair):
    return (ctf_rows[:, :, None] * spectrum(images, forward_pair)).astype(jnp.bfloat16)


def prior_term(prior_angle, angle_count):
    rotations = jnp.arange(angle_count, dtype=jnp.int32)
    offsets = (rotations[None, :] - prior_angle[:, None]) % angle_count
    return prior_strength * jnp.cos(offsets.astype(jnp.float32) * (2.0 * math.pi / angle_count))


def pair_refs(spec_four):
    cos_part = spec_four[:, :, 0]
    sin_part = spec_four[:, :, 1]
    first_pair = jnp.stack([cos_part, sin_part], axis=2)
    second_pair = jnp.stack([-sin_part, cos_part], axis=2)
    return jnp.stack([first_pair, second_pair], axis=1)


def pair_weights(spec_four):
    cos_part = spec_four[:, :, 0]
    sin_part = spec_four[:, :, 1]
    first_pair = jnp.stack([cos_part, sin_part], axis=2)
    second_pair = jnp.stack([-sin_part, cos_part], axis=2)
    return jnp.stack([first_pair, second_pair], axis=2)


def local(images, class_refs, ctf_table, ctf_group, prior_angle, precision):
    particle_count, cycle_count, angle_count = images.shape
    mode_count = angle_count // 2
    class_count = class_refs.shape[0]
    forward = angle_table(angle_count, mode_count)
    forward_pair = split_table(forward)
    synthesis = synthesis_table(angle_count, mode_count)
    ref_local = spectrum(class_refs, forward_pair).astype(jnp.bfloat16)
    ref_spectra = lax.all_gather(ref_local, "dom", axis=1, tiled=True)
    group_ids = jnp.arange(ctf_table.shape[0], dtype=jnp.int32)
    one_hot = (ctf_group[:, None] == group_ids[None, :]).astype(jnp.float32)
    ctf_rows = jnp.dot(one_hot, ctf_table, precision=highest, preferred_element_type=jnp.float32)
    ctf_square = ctf_rows * ctf_rows
    particle_spectra = weighted_spectrum(images, ctf_rows, forward_pair)
    ref_float = ref_spectra.astype(jnp.float32)
    cycle_energy = jnp.sum(ref_float * ref_float * mode_weights(angle_count, mode_count), axis=2)
    energy = jnp.dot(
        ctf_square,
        jnp.transpose(cycle_energy),
        precision=highest,
        preferred_element_type=jnp.float32,
    )
    particle_four = particle_spectra.reshape(particle_count, cycle_count, 2, mode_count)
    ref_pairs = pair_refs(ref_spectra.reshape(class_count, cycle_count, 2, mode_count))
    cross = jnp.einsum(
        "prhm,kjrhm->pkjm", particle_four, ref_pairs, preferred_element_type=jnp.float32
    )
    correlation = jnp.dot(
        cross.reshape(-1, angle_count),
        synthesis,
        precision=highest,
        preferred_element_type=jnp.float32,
    )
    correlation = correlation.reshape(particle_count, class_count, angle_count)
    score = precision[:, None, None] * (correlation - 0.5 * energy[:, :, None])
    score = score + prior_term(prior_angle, angle_count)[:, None, :]
    row_top = jnp.max(score, axis=(1, 2))
    peak = lax.pmax(row_top, "cls")
    local_sum = jnp.sum(jnp.exp(score - peak[:, None, None]), axis=(1, 2))
    sum_exp = lax.psum(local_sum, "cls")
    log_evidence = peak + jnp.log(sum_exp)
    weights = jnp.exp(score - log_evidence[:, None, None]).astype(jnp.bfloat16)
    weight_spectra = spectrum(weights, forward_pair).astype(jnp.bfloat16)
    mass = jnp.sum(weights.astype(jnp.float32), axis=2)
    weight_pairs = pair_weights(weight_spectra.reshape(particle_count, class_count, 2, mode_count))
    class_sums = jnp.einsum(
        "pkjhm,prhm->rkjm", weight_pairs, particle_four, preferred_element_type=jnp.float32
    )
    class_sums = class_sums.reshape(cycle_count, class_count, angle_count)
    totals = jnp.dot(
        jnp.transpose(ctf_square), mass, precision=highest, preferred_element_type=jnp.float32
    )
    whole_sums, whole_totals = lax.psum((class_sums, totals), "dom")
    cycle_share = cycle_count // lax.axis_size("dom")
    cycle_start = lax.axis_index("dom") * cycle_share
    cycle_sums = lax.dynamic_slice_in_dim(whole_sums, cycle_start, cycle_share, 0)
    cycle_totals = lax.dynamic_slice_in_dim(whole_totals, cycle_start, cycle_share, 0)
    new_spectra = cycle_sums / (cycle_totals + ridge)[:, :, None]
    new_refs = jnp.dot(
        new_spectra.reshape(-1, angle_count),
        synthesis,
        precision=highest,
        preferred_element_type=jnp.float32,
    )
    new_refs = jnp.transpose(
        new_refs.reshape(cycle_sums.shape[0], class_count, angle_count), (1, 0, 2)
    )
    return (new_refs, log_evidence)


gap = 8


def block_at(index, size):
    return slice(index * (size + gap), index * (size + gap) + size)


def nt(left, right, precision=None):
    return lax.dot_general(
        left,
        right,
        (((1,), (1,)), ((), ())),
        precision=precision,
        preferred_element_type=jnp.float32,
    )


def nn(left, right, precision=None):
    return jnp.dot(left, right, precision=precision, preferred_element_type=jnp.float32)


def halves(value):
    upper = value.astype(jnp.bfloat16)
    lower = (value - upper.astype(jnp.float32)).astype(jnp.bfloat16)
    return upper, lower


def rounded(value):
    return value.astype(jnp.bfloat16).astype(jnp.float32)


def host_tables(angle_count, mode_count):
    product = np.outer(np.arange(angle_count), np.arange(mode_count)) % angle_count
    phase = product * (2.0 * math.pi / angle_count)
    forward = np.concatenate([np.cos(phase), np.sin(phase)], axis=1).astype(np.float32)
    single = np.where(np.arange(mode_count) == 0, 1.0, 2.0) / angle_count
    scale = np.concatenate([single, single]).astype(np.float32)
    inverse = forward * scale[None, :]

    def split(table):
        upper = table.astype(ml_dtypes.bfloat16)
        lower = (table - upper.astype(np.float32)).astype(ml_dtypes.bfloat16)
        return upper, lower

    return split(np.ascontiguousarray(forward.T)) + split(inverse)


def whole_kernel(
    dom_size, cls_size, img, refs, table, group, angle, prec, fwd_hi, fwd_lo, inv_hi, inv_lo,
    out_new, out_log, ref_slots, ref_rows, ctf, spec, ref_spec, cross, score, sums, send, recv,
    tot_send, tot_recv, stat_send, stat_recv, ref_sems, stat_sems, sum_sems, tot_sems,
):
    mesh_ids = pl.DeviceIdType.MESH
    dom, cls = lax.axis_index("dom"), lax.axis_index("cls")
    parts, cycles, angles = img.shape
    modes = angles // 2
    share = cycles // dom_size
    classes = refs.shape[0] // share
    barrier = pltpu.get_barrier_semaphore()
    for step in range(1, dom_size):
        pl.semaphore_signal(barrier, inc=1, device_id={"dom": lax.rem(dom + step, dom_size)}, device_id_type=mesh_ids)
    for step in range(1, cls_size):
        pl.semaphore_signal(barrier, inc=1, device_id={"cls": lax.rem(cls + step, cls_size)}, device_id_type=mesh_ids)

    def remote(source, target, sems, axis, place, size, step):
        return pltpu.make_async_remote_copy(
            src_ref=source,
            dst_ref=target,
            send_sem=sems.at[0, step],
            recv_sem=sems.at[1, step],
            device_id={axis: lax.rem(place + step, size)},
            device_id_type=mesh_ids,
        )

    ref_copies = [
        remote(refs, ref_slots.at[step], ref_sems, "dom", dom, dom_size, step)
        for step in range(1, dom_size)
    ]
    lanes = lax.broadcasted_iota(jnp.int32, (modes, modes), 1)
    low = lanes < cycles
    groups = lax.broadcasted_iota(jnp.int32, (parts, table.shape[0]), 1)
    one_hot = (groups == group[...]).astype(jnp.float32)
    ctf[...] = nn(one_hot, table[...], highest)

    def transform(block):
        result = nt(fwd_hi[...], block) + nt(fwd_lo[...], block)
        found = []
        for pair in range(2):
            top = result[:modes, pair * modes : (pair + 1) * modes]
            bottom = result[modes:, pair * modes : (pair + 1) * modes]
            found.append(jnp.where(low, top, pltpu.roll(bottom, cycles, 1)))
            found.append(jnp.where(low, pltpu.roll(top, cycles, 1), bottom))
        return found

    def image_step(step, carry):
        first = step * 4
        block = img[pl.ds(first, 4)].reshape(4 * cycles, angles)
        for offset, value in enumerate(transform(block)):
            row = ctf[pl.ds(first + offset, 1), :]
            spec[pl.ds(first + offset, modes, stride=parts + gap), :] = value * row
        return carry

    early = parts // 16
    lax.fori_loop(0, early, image_step, 0, unroll=4)
    pl.semaphore_wait(barrier, dom_size + cls_size - 2)
    for copy in ref_copies:
        copy.start()
    lax.fori_loop(early, parts // 4, image_step, 0, unroll=4)

    turns = lax.broadcasted_iota(jnp.int32, (angles, parts), 0)
    offsets = (turns - angle[...] + angles) % angles
    prior = prior_strength * jnp.cos(offsets.astype(jnp.float32) * (2.0 * math.pi / angles))

    for copy in ref_copies:
        copy.wait()
    for step in range(dom_size):
        source = refs[...] if step == 0 else ref_slots[step]
        source = source.astype(jnp.float32).reshape(classes, share, angles)
        owner = lax.rem(dom - step + dom_size, dom_size)
        ref_rows[:, pl.ds(pl.multiple_of(owner * share, share), share), :] = source
    rows = lax.broadcasted_iota(jnp.int32, (modes, modes), 0)
    weight = jnp.where(rows == 0, 1.0, 2.0) * (1.0 / angles)
    sign = jnp.where(lax.broadcasted_iota(jnp.int32, (classes, modes), 1) < cycles, 1.0, -1.0)
    energies = []
    for step in range(classes // 4):
        block = ref_rows[step * 4 : step * 4 + 4].reshape(4 * cycles, angles).astype(jnp.bfloat16)
        for offset, value in enumerate(transform(block)):
            index = step * 4 + offset
            value = rounded(value)
            energies.append(jnp.sum(value * value * weight, axis=0, keepdims=True))
            ref_spec[pl.ds(index, modes, stride=2 * classes + gap), :] = value
            turned = pltpu.roll(value, cycles, 1)
            ref_spec[pl.ds(classes + index, modes, stride=2 * classes + gap), :] = jnp.where(low, -turned, turned)
    ctf_square = ctf[...] * ctf[...]
    energy = nt(jnp.concatenate(energies, axis=0), ctf_square, highest)

    def cross_step(mode, carry):
        particles = spec[pl.ds(pl.multiple_of(mode * (parts + gap), gap), parts), :].astype(jnp.bfloat16)
        others = ref_spec[pl.ds(pl.multiple_of(mode * (2 * classes + gap), gap), 2 * classes), :]
        cross[pl.ds(mode, 2 * classes, stride=modes + gap), :] = nt(others.astype(jnp.bfloat16), particles)
        return carry

    lax.fori_loop(0, modes, cross_step, 0, unroll=32)

    scale = prec[...]
    peak = None
    for index in range(classes):
        both = jnp.concatenate(
            [cross[block_at(index, modes), :],
             cross[block_at(classes + index, modes), :]], axis=0)
        upper, lower = halves(both)
        found = nn(inv_hi[...], upper) + (nn(inv_hi[...], lower) + nn(inv_lo[...], upper))
        found = scale * (found - 0.5 * energy[index : index + 1, :]) + prior
        score[index] = found
        top = jnp.max(found, axis=0, keepdims=True)
        peak = top if peak is None else jnp.maximum(peak, top)
    total = jnp.zeros((1, parts), jnp.float32)
    for index in range(classes):
        total = total + jnp.sum(jnp.exp(score[index] - peak), axis=0, keepdims=True)
    stat_send[...] = jnp.concatenate([peak] * 4 + [total] * 4, axis=0)
    stat_copies = [
        remote(stat_send, stat_recv.at[step], stat_sems, "cls", cls, cls_size, step)
        for step in range(1, cls_size)
    ]
    for copy in stat_copies:
        copy.start()
    for copy in stat_copies:
        copy.wait()
    pairs = [(peak, total)]
    for step in range(1, cls_size):
        pairs.append((stat_recv[step, 0:1, :], stat_recv[step, 4:5, :]))
    best = peak
    for other, _ in pairs[1:]:
        best = jnp.maximum(best, other)
    whole = jnp.zeros((1, parts), jnp.float32)
    for other, part in pairs:
        whole = whole + part * jnp.exp(other - best)
    log_evidence = best + jnp.log(whole)
    out_log[...] = log_evidence

    masses = []
    for index in range(classes):
        weights = jnp.exp(score[index] - log_evidence).astype(jnp.bfloat16)
        masses.append(jnp.sum(weights.astype(jnp.float32), axis=0, keepdims=True))
        found = nn(fwd_hi[...], weights) + nn(fwd_lo[...], weights)
        cross[block_at(index, modes), :] = found[:modes]
        cross[block_at(classes + index, modes), :] = found[modes:]
    tot_send[...] = nn(jnp.concatenate(masses, axis=0), ctf_square, highest)
    tot_copies = [
        remote(tot_send, tot_recv.at[step], tot_sems, "dom", dom, dom_size, step)
        for step in range(1, dom_size)
    ]
    for copy in tot_copies:
        copy.start()

    def sum_step(mode, carry):
        particles = spec[pl.ds(pl.multiple_of(mode * (parts + gap), gap), parts), :].astype(jnp.bfloat16)
        weights = cross[pl.ds(mode, 2 * classes, stride=modes + gap), :].astype(jnp.bfloat16)
        found = nn(weights, particles)
        found = found[:classes] + sign * pltpu.roll(found[classes:], cycles, 1)
        sums[pl.ds(mode, classes, stride=modes + gap), :] = found
        return carry

    lax.fori_loop(0, modes, sum_step, 0, unroll=32)

    for index in range(classes):
        turned = jnp.transpose(sums[block_at(index, modes), :])
        for part in range(dom_size):
            piece = jnp.concatenate(
                [turned[part * share : (part + 1) * share],
                 turned[cycles + part * share : cycles + (part + 1) * share]], axis=0)
            send[part, index * 2 * share : (index + 1) * 2 * share, :] = piece.astype(jnp.bfloat16)
    sum_copies = [
        remote(send.at[lax.rem(dom + step, dom_size)], recv.at[step], sum_sems, "dom", dom, dom_size, step)
        for step in range(1, dom_size)
    ]
    for copy in sum_copies:
        copy.start()
    for copy in tot_copies:
        copy.wait()
    totals = tot_send[...]
    for step in range(1, dom_size):
        totals = totals + tot_recv[step]
    columns = lax.broadcasted_iota(jnp.int32, (1, share, modes), 2)
    wanted = lax.broadcasted_iota(jnp.int32, (1, share, modes), 1) + dom * share
    picked = jnp.where(columns == wanted, totals[:, None, :], 0.0)
    divisor = jnp.sum(picked, axis=2, keepdims=True).reshape(classes * share, 1) + ridge
    for copy in sum_copies:
        copy.wait()
    gathered = send[dom].astype(jnp.float32)
    for step in range(1, dom_size):
        gathered = gathered + recv[step].astype(jnp.float32)
    gathered = gathered.reshape(classes, 2, share, modes)
    result = jnp.zeros((classes * share, angles), jnp.float32)
    for half in range(2):
        upper, lower = halves(gathered[:, half].reshape(classes * share, modes))
        hi = inv_hi[:, half * modes : (half + 1) * modes]
        lo = inv_lo[:, half * modes : (half + 1) * modes]
        result = result + nt(upper, hi) + (nt(lower, hi) + nt(upper, lo))
    out_new[...] = result / divisor


def fused(images, class_refs, ctf_table, ctf_group, prior_angle, precision):
    dom_size, cls_size = lax.axis_size("dom"), lax.axis_size("cls")
    parts, cycles, angles = images.shape
    modes = angles // 2
    classes, share, _ = class_refs.shape
    tables = host_tables(angles, modes)
    f32, bf16 = jnp.float32, jnp.bfloat16
    vmem = pl.BlockSpec(memory_space=pltpu.VMEM)
    new_refs, log_evidence = pl.pallas_call(
        functools.partial(whole_kernel, dom_size, cls_size),
        out_shape=(
            jax.ShapeDtypeStruct((classes * share, angles), f32),
            jax.ShapeDtypeStruct((1, parts), f32),
        ),
        in_specs=[vmem] * 10,
        out_specs=(vmem, vmem),
        scratch_shapes=[
            pltpu.VMEM((dom_size, classes * share, angles), bf16),
            pltpu.VMEM((classes, cycles, angles), f32),
            pltpu.VMEM((parts, modes), f32),
            pltpu.VMEM((modes * (parts + gap), modes), f32),
            pltpu.VMEM((modes * (2 * classes + gap), modes), f32),
            pltpu.VMEM((2 * classes * (modes + gap), parts), f32),
            pltpu.VMEM((classes, angles, parts), f32),
            pltpu.VMEM((classes * (modes + gap), modes), f32),
            pltpu.VMEM((dom_size, classes * 2 * share, modes), bf16),
            pltpu.VMEM((dom_size, classes * 2 * share, modes), bf16),
            pltpu.VMEM((classes, modes), f32),
            pltpu.VMEM((dom_size, classes, modes), f32),
            pltpu.VMEM((8, parts), f32),
            pltpu.VMEM((cls_size, 8, parts), f32),
            pltpu.SemaphoreType.DMA((2, dom_size)),
            pltpu.SemaphoreType.DMA((2, cls_size)),
            pltpu.SemaphoreType.DMA((2, dom_size)),
            pltpu.SemaphoreType.DMA((2, dom_size)),
        ],
        compiler_params=pltpu.CompilerParams(
            collective_id=0, has_side_effects=True, vmem_limit_bytes=52 * 1024 * 1024
        ),
    )(
        images,
        class_refs.reshape(classes * share, angles),
        jnp.concatenate([ctf_table, ctf_table], axis=1),
        ctf_group[:, None],
        prior_angle[None, :],
        precision[None, :],
        *[jnp.asarray(table) for table in tables],
    )
    return new_refs.reshape(classes, share, angles), log_evidence.reshape(parts)


def pick(images, class_refs, *rest):
    parts, cycles, angles = images.shape
    classes, share, _ = class_refs.shape
    fits = angles == 256 and cycles == 64 and parts == 128 and share % 8 == 0 and classes % 16 == 0
    return (fused if fits else local)(images, class_refs, *rest)


def solution(mesh):
    in_specs = (P("dom", None, None), P("cls", "dom", None), P(), P("dom"), P("dom"), P("dom"))
    out_specs = (P("cls", "dom", None), P("dom"))
    return jax.shard_map(pick, mesh=mesh, in_specs=in_specs, out_specs=out_specs, check_vma=False)
```

```python
import functools
import math

import jax
import jax.numpy as jnp
import ml_dtypes
import numpy as np
from jax import lax
from jax.experimental import pallas as pl
from jax.experimental.pallas import tpu as pltpu
from jax.sharding import PartitionSpec as P

prior_strength = 2.0
ridge = 1.0
highest = lax.Precision.HIGHEST


def angle_table(angle_count, mode_count):
    angles = jnp.arange(angle_count, dtype=jnp.int32)
    freqs = jnp.arange(mode_count, dtype=jnp.int32)
    product = angles[:, None] * freqs[None, :] % angle_count
    phase = product.astype(jnp.float32) * (2.0 * math.pi / angle_count)
    return jnp.concatenate([jnp.cos(phase), jnp.sin(phase)], axis=1)


def split_table(forward):
    upper = forward.astype(jnp.bfloat16)
    lower = (forward - upper.astype(jnp.float32)).astype(jnp.bfloat16)
    return (upper, lower)


def mode_weights(angle_count, mode_count):
    freqs = jnp.arange(mode_count, dtype=jnp.int32)
    single = jnp.where(freqs == 0, 1.0, 2.0).astype(jnp.float32) / angle_count
    return jnp.concatenate([single, single])


def synthesis_table(angle_count, mode_count):
    return (
        jnp.transpose(angle_table(angle_count, mode_count))
        * mode_weights(angle_count, mode_count)[:, None]
    )


def spectrum(values, forward_pair):
    upper, lower = forward_pair
    flat = values.reshape(-1, values.shape[-1])
    result = jnp.dot(flat, upper, preferred_element_type=jnp.float32)
    result = result + jnp.dot(flat, lower, preferred_element_type=jnp.float32)
    return result.reshape(values.shape[:-1] + (upper.shape[1],))


def weighted_spectrum(images, ctf_rows, forward_pair):
    return (ctf_rows[:, :, None] * spectrum(images, forward_pair)).astype(jnp.bfloat16)


def prior_term(prior_angle, angle_count):
    rotations = jnp.arange(angle_count, dtype=jnp.int32)
    offsets = (rotations[None, :] - prior_angle[:, None]) % angle_count
    return prior_strength * jnp.cos(offsets.astype(jnp.float32) * (2.0 * math.pi / angle_count))


def pair_refs(spec_four):
    cos_part = spec_four[:, :, 0]
    sin_part = spec_four[:, :, 1]
    first_pair = jnp.stack([cos_part, sin_part], axis=2)
    second_pair = jnp.stack([-sin_part, cos_part], axis=2)
    return jnp.stack([first_pair, second_pair], axis=1)


def pair_weights(spec_four):
    cos_part = spec_four[:, :, 0]
    sin_part = spec_four[:, :, 1]
    first_pair = jnp.stack([cos_part, sin_part], axis=2)
    second_pair = jnp.stack([-sin_part, cos_part], axis=2)
    return jnp.stack([first_pair, second_pair], axis=2)


def local(images, class_refs, ctf_table, ctf_group, prior_angle, precision):
    particle_count, cycle_count, angle_count = images.shape
    mode_count = angle_count // 2
    class_count = class_refs.shape[0]
    forward = angle_table(angle_count, mode_count)
    forward_pair = split_table(forward)
    synthesis = synthesis_table(angle_count, mode_count)
    ref_local = spectrum(class_refs, forward_pair).astype(jnp.bfloat16)
    ref_spectra = lax.all_gather(ref_local, "dom", axis=1, tiled=True)
    group_ids = jnp.arange(ctf_table.shape[0], dtype=jnp.int32)
    one_hot = (ctf_group[:, None] == group_ids[None, :]).astype(jnp.float32)
    ctf_rows = jnp.dot(one_hot, ctf_table, precision=highest, preferred_element_type=jnp.float32)
    ctf_square = ctf_rows * ctf_rows
    particle_spectra = weighted_spectrum(images, ctf_rows, forward_pair)
    ref_float = ref_spectra.astype(jnp.float32)
    cycle_energy = jnp.sum(ref_float * ref_float * mode_weights(angle_count, mode_count), axis=2)
    energy = jnp.dot(
        ctf_square,
        jnp.transpose(cycle_energy),
        precision=highest,
        preferred_element_type=jnp.float32,
    )
    particle_four = particle_spectra.reshape(particle_count, cycle_count, 2, mode_count)
    ref_pairs = pair_refs(ref_spectra.reshape(class_count, cycle_count, 2, mode_count))
    cross = jnp.einsum(
        "prhm,kjrhm->pkjm", particle_four, ref_pairs, preferred_element_type=jnp.float32
    )
    correlation = jnp.dot(
        cross.reshape(-1, angle_count),
        synthesis,
        precision=highest,
        preferred_element_type=jnp.float32,
    )
    correlation = correlation.reshape(particle_count, class_count, angle_count)
    score = precision[:, None, None] * (correlation - 0.5 * energy[:, :, None])
    score = score + prior_term(prior_angle, angle_count)[:, None, :]
    row_top = jnp.max(score, axis=(1, 2))
    peak = lax.pmax(row_top, "cls")
    local_sum = jnp.sum(jnp.exp(score - peak[:, None, None]), axis=(1, 2))
    sum_exp = lax.psum(local_sum, "cls")
    log_evidence = peak + jnp.log(sum_exp)
    weights = jnp.exp(score - log_evidence[:, None, None]).astype(jnp.bfloat16)
    weight_spectra = spectrum(weights, forward_pair).astype(jnp.bfloat16)
    mass = jnp.sum(weights.astype(jnp.float32), axis=2)
    weight_pairs = pair_weights(weight_spectra.reshape(particle_count, class_count, 2, mode_count))
    class_sums = jnp.einsum(
        "pkjhm,prhm->rkjm", weight_pairs, particle_four, preferred_element_type=jnp.float32
    )
    class_sums = class_sums.reshape(cycle_count, class_count, angle_count)
    totals = jnp.dot(
        jnp.transpose(ctf_square), mass, precision=highest, preferred_element_type=jnp.float32
    )
    whole_sums, whole_totals = lax.psum((class_sums, totals), "dom")
    cycle_share = cycle_count // lax.axis_size("dom")
    cycle_start = lax.axis_index("dom") * cycle_share
    cycle_sums = lax.dynamic_slice_in_dim(whole_sums, cycle_start, cycle_share, 0)
    cycle_totals = lax.dynamic_slice_in_dim(whole_totals, cycle_start, cycle_share, 0)
    new_spectra = cycle_sums / (cycle_totals + ridge)[:, :, None]
    new_refs = jnp.dot(
        new_spectra.reshape(-1, angle_count),
        synthesis,
        precision=highest,
        preferred_element_type=jnp.float32,
    )
    new_refs = jnp.transpose(
        new_refs.reshape(cycle_sums.shape[0], class_count, angle_count), (1, 0, 2)
    )
    return (new_refs, log_evidence)


gap = 8


def block_at(index, size):
    return slice(index * (size + gap), index * (size + gap) + size)


def nt(left, right, precision=None):
    return lax.dot_general(
        left,
        right,
        (((1,), (1,)), ((), ())),
        precision=precision,
        preferred_element_type=jnp.float32,
    )


def nn(left, right, precision=None):
    return jnp.dot(left, right, precision=precision, preferred_element_type=jnp.float32)


def halves(value):
    upper = value.astype(jnp.bfloat16)
    lower = (value - upper.astype(jnp.float32)).astype(jnp.bfloat16)
    return upper, lower


def rounded(value):
    return value.astype(jnp.bfloat16).astype(jnp.float32)


def host_tables(angle_count, mode_count):
    product = np.outer(np.arange(angle_count), np.arange(mode_count)) % angle_count
    phase = product * (2.0 * math.pi / angle_count)
    forward = np.concatenate([np.cos(phase), np.sin(phase)], axis=1).astype(np.float32)
    single = np.where(np.arange(mode_count) == 0, 1.0, 2.0) / angle_count
    scale = np.concatenate([single, single]).astype(np.float32)
    inverse = forward * scale[None, :]

    def split(table):
        upper = table.astype(ml_dtypes.bfloat16)
        lower = (table - upper.astype(np.float32)).astype(ml_dtypes.bfloat16)
        return upper, lower

    return split(np.ascontiguousarray(forward.T)) + split(inverse)


def whole_kernel(
    dom_size, cls_size, img_in, refs_in, table_in, group_in, angle_in, prec_in, fwd_hi_in, fwd_lo_in, inv_hi_in, inv_lo_in,
    out_new, out_log, ref_slots, ref_rows, ctf, spec, ref_spec, cross, score, sums, send, recv,
    tot_send, tot_recv, stat_send, stat_recv, img, table, group, angle, prec, fwd_hi, fwd_lo, inv_hi, inv_lo, load_sems, ref_sems, stat_sems, sum_sems, tot_sems,
):
    mesh_ids = pl.DeviceIdType.MESH
    dom, cls = lax.axis_index("dom"), lax.axis_index("cls")
    parts, cycles, angles = img_in.shape
    modes = angles // 2
    share = cycles // dom_size
    classes = refs_in.shape[0] // share
    barrier = pltpu.get_barrier_semaphore()
    for step in range(1, dom_size):
        pl.semaphore_signal(barrier, inc=1, device_id={"dom": lax.rem(dom + step, dom_size)}, device_id_type=mesh_ids)
    for step in range(1, cls_size):
        pl.semaphore_signal(barrier, inc=1, device_id={"cls": lax.rem(cls + step, cls_size)}, device_id_type=mesh_ids)

    early = parts // 16
    pieces = [pl.ds(start, early * 4) for start in range(0, parts, early * 4)]
    small = [
        (table_in, table), (group_in, group), (fwd_hi_in, fwd_hi), (fwd_lo_in, fwd_lo),
        (img_in.at[pieces[0]], img.at[pieces[0]]),
    ]
    late = [(img_in.at[piece], img.at[piece]) for piece in pieces[1:]] + [
        (angle_in, angle), (prec_in, prec), (inv_hi_in, inv_hi), (inv_lo_in, inv_lo), (refs_in, ref_slots.at[0])
    ]
    loads = [
        pltpu.make_async_copy(source, target, load_sems.at[place])
        for place, (source, target) in enumerate(small + late)
    ]
    for load in loads:
        load.start()

    def remote(source, target, sems, axis, place, size, step):
        return pltpu.make_async_remote_copy(
            src_ref=source,
            dst_ref=target,
            send_sem=sems.at[0, step],
            recv_sem=sems.at[1, step],
            device_id={axis: lax.rem(place + step, size)},
            device_id_type=mesh_ids,
        )

    ref_copies = [
        remote(refs_in, ref_slots.at[step], ref_sems, "dom", dom, dom_size, step)
        for step in range(1, dom_size)
    ]
    lanes = lax.broadcasted_iota(jnp.int32, (modes, modes), 1)
    low = lanes < cycles
    for load in loads[: len(small)]:
        load.wait()
    groups = lax.broadcasted_iota(jnp.int32, (table.shape[0], parts), 0)
    one_hot = (groups == group[...]).astype(jnp.float32)
    doubled = jnp.concatenate([table[...], table[...]], axis=1)
    ctf[...] = lax.dot_general(
        one_hot, doubled, (((0,), (0,)), ((), ())), precision=highest, preferred_element_type=jnp.float32
    )

    def transform(block):
        result = nt(fwd_hi[...], block) + nt(fwd_lo[...], block)
        found = []
        for pair in range(2):
            top = result[:modes, pair * modes : (pair + 1) * modes]
            bottom = result[modes:, pair * modes : (pair + 1) * modes]
            found.append(jnp.where(low, top, pltpu.roll(bottom, cycles, 1)))
            found.append(jnp.where(low, pltpu.roll(top, cycles, 1), bottom))
        return found

    def image_step(step, carry):
        first = step * 4
        block = img[pl.ds(first, 4)].reshape(4 * cycles, angles)
        for offset, value in enumerate(transform(block)):
            row = ctf[pl.ds(first + offset, 1), :]
            spec[pl.ds(first + offset, modes, stride=parts + gap), :] = value * row
        return carry

    lax.fori_loop(0, early, image_step, 0, unroll=4)
    pl.semaphore_wait(barrier, dom_size + cls_size - 2)
    for copy in ref_copies:
        copy.start()
    for load in loads[len(small) :]:
        load.wait()
    lax.fori_loop(early, parts // 4, image_step, 0, unroll=4)

    turns = lax.broadcasted_iota(jnp.int32, (angles, parts), 0)
    offsets = (turns - angle[...] + angles) % angles
    prior = prior_strength * jnp.cos(offsets.astype(jnp.float32) * (2.0 * math.pi / angles))

    for copy in ref_copies:
        copy.wait()
    for step in range(dom_size):
        source = ref_slots[step].astype(jnp.float32).reshape(classes, share, angles)
        owner = lax.rem(dom - step + dom_size, dom_size)
        ref_rows[:, pl.ds(pl.multiple_of(owner * share, share), share), :] = source
    rows = lax.broadcasted_iota(jnp.int32, (modes, modes), 0)
    weight = jnp.where(rows == 0, 1.0, 2.0) * (1.0 / angles)
    sign = jnp.where(lax.broadcasted_iota(jnp.int32, (classes, modes), 1) < cycles, 1.0, -1.0)
    energies = []
    for step in range(classes // 4):
        block = ref_rows[step * 4 : step * 4 + 4].reshape(4 * cycles, angles).astype(jnp.bfloat16)
        for offset, value in enumerate(transform(block)):
            index = step * 4 + offset
            value = rounded(value)
            energies.append(jnp.sum(value * value * weight, axis=0, keepdims=True))
            ref_spec[pl.ds(index, modes, stride=2 * classes + gap), :] = value
            turned = pltpu.roll(value, cycles, 1)
            ref_spec[pl.ds(classes + index, modes, stride=2 * classes + gap), :] = jnp.where(low, -turned, turned)
    ctf_square = ctf[...] * ctf[...]
    energy = nt(jnp.concatenate(energies, axis=0), ctf_square, highest)

    def cross_step(mode, carry):
        particles = spec[pl.ds(pl.multiple_of(mode * (parts + gap), gap), parts), :].astype(jnp.bfloat16)
        others = ref_spec[pl.ds(pl.multiple_of(mode * (2 * classes + gap), gap), 2 * classes), :]
        cross[pl.ds(mode, 2 * classes, stride=modes + gap), :] = nt(others.astype(jnp.bfloat16), particles)
        return carry

    lax.fori_loop(0, modes, cross_step, 0, unroll=64)

    scale = prec[...]
    peak = None
    for index in range(classes):
        both = jnp.concatenate(
            [cross[block_at(index, modes), :],
             cross[block_at(classes + index, modes), :]], axis=0)
        upper, lower = halves(both)
        found = nn(inv_hi[...], upper) + (nn(inv_hi[...], lower) + nn(inv_lo[...], upper))
        found = scale * (found - 0.5 * energy[index : index + 1, :]) + prior
        score[index] = found
        top = jnp.max(found, axis=0, keepdims=True)
        peak = top if peak is None else jnp.maximum(peak, top)
    total = jnp.zeros((1, parts), jnp.float32)
    for index in range(classes):
        total = total + jnp.sum(jnp.exp(score[index] - peak), axis=0, keepdims=True)
    stat_send[...] = jnp.concatenate([peak] * 4 + [total] * 4, axis=0)
    stat_copies = [
        remote(stat_send, stat_recv.at[step], stat_sems, "cls", cls, cls_size, step)
        for step in range(1, cls_size)
    ]
    for copy in stat_copies:
        copy.start()
    for copy in stat_copies:
        copy.wait()
    pairs = [(peak, total)]
    for step in range(1, cls_size):
        pairs.append((stat_recv[step, 0:1, :], stat_recv[step, 4:5, :]))
    best = peak
    for other, _ in pairs[1:]:
        best = jnp.maximum(best, other)
    whole = jnp.zeros((1, parts), jnp.float32)
    for other, part in pairs:
        whole = whole + part * jnp.exp(other - best)
    log_evidence = best + jnp.log(whole)
    out_log[...] = log_evidence

    masses = []
    for index in range(classes):
        weights = jnp.exp(score[index] - log_evidence).astype(jnp.bfloat16)
        masses.append(jnp.sum(weights.astype(jnp.float32), axis=0, keepdims=True))
        found = nn(fwd_hi[...], weights) + nn(fwd_lo[...], weights)
        cross[block_at(index, modes), :] = found[:modes]
        cross[block_at(classes + index, modes), :] = found[modes:]
    tot_send[...] = nn(jnp.concatenate(masses, axis=0), ctf_square, highest)
    tot_copies = [
        remote(tot_send, tot_recv.at[step], tot_sems, "dom", dom, dom_size, step)
        for step in range(1, dom_size)
    ]
    for copy in tot_copies:
        copy.start()

    def sum_step(mode, carry):
        particles = spec[pl.ds(pl.multiple_of(mode * (parts + gap), gap), parts), :].astype(jnp.bfloat16)
        weights = cross[pl.ds(mode, 2 * classes, stride=modes + gap), :].astype(jnp.bfloat16)
        found = nn(weights, particles)
        found = found[:classes] + sign * pltpu.roll(found[classes:], cycles, 1)
        sums[pl.ds(mode, classes, stride=modes + gap), :] = found
        return carry

    lax.fori_loop(0, modes, sum_step, 0, unroll=64)

    for index in range(classes):
        turned = jnp.transpose(sums[block_at(index, modes), :])
        for part in range(dom_size):
            piece = jnp.concatenate(
                [turned[part * share : (part + 1) * share],
                 turned[cycles + part * share : cycles + (part + 1) * share]], axis=0)
            send[part, index * 2 * share : (index + 1) * 2 * share, :] = piece.astype(jnp.bfloat16)
    sum_copies = [
        remote(send.at[lax.rem(dom + step, dom_size)], recv.at[step], sum_sems, "dom", dom, dom_size, step)
        for step in range(1, dom_size)
    ]
    for copy in sum_copies:
        copy.start()
    for copy in tot_copies:
        copy.wait()
    totals = tot_send[...]
    for step in range(1, dom_size):
        totals = totals + tot_recv[step]
    columns = lax.broadcasted_iota(jnp.int32, (1, share, modes), 2)
    wanted = lax.broadcasted_iota(jnp.int32, (1, share, modes), 1) + dom * share
    picked = jnp.where(columns == wanted, totals[:, None, :], 0.0)
    divisor = jnp.sum(picked, axis=2, keepdims=True).reshape(classes * share, 1) + ridge
    for copy in sum_copies:
        copy.wait()
    gathered = send[dom].astype(jnp.float32)
    for step in range(1, dom_size):
        gathered = gathered + recv[step].astype(jnp.float32)
    gathered = gathered.reshape(classes, 2, share, modes)
    result = jnp.zeros((classes * share, angles), jnp.float32)
    for half in range(2):
        upper, lower = halves(gathered[:, half].reshape(classes * share, modes))
        hi = inv_hi[:, half * modes : (half + 1) * modes]
        lo = inv_lo[:, half * modes : (half + 1) * modes]
        result = result + nt(upper, hi) + (nt(lower, hi) + nt(upper, lo))
    out_new[...] = result / divisor


def fused(images, class_refs, ctf_table, ctf_group, prior_angle, precision):
    dom_size, cls_size = lax.axis_size("dom"), lax.axis_size("cls")
    parts, cycles, angles = images.shape
    modes = angles // 2
    classes, share, _ = class_refs.shape
    tables = host_tables(angles, modes)
    f32, bf16 = jnp.float32, jnp.bfloat16
    vmem = pl.BlockSpec(memory_space=pltpu.VMEM)
    new_refs, log_evidence = pl.pallas_call(
        functools.partial(whole_kernel, dom_size, cls_size),
        out_shape=(
            jax.ShapeDtypeStruct((classes * share, angles), f32),
            jax.ShapeDtypeStruct((1, parts), f32),
        ),
        in_specs=[pl.BlockSpec(memory_space=pltpu.HBM)] * 10,
        out_specs=(vmem, vmem),
        scratch_shapes=[
            pltpu.VMEM((dom_size, classes * share, angles), bf16),
            pltpu.VMEM((classes, cycles, angles), f32),
            pltpu.VMEM((parts, modes), f32),
            pltpu.VMEM((modes * (parts + gap), modes), f32),
            pltpu.VMEM((modes * (2 * classes + gap), modes), f32),
            pltpu.VMEM((2 * classes * (modes + gap), parts), f32),
            pltpu.VMEM((classes, angles, parts), f32),
            pltpu.VMEM((classes * (modes + gap), modes), f32),
            pltpu.VMEM((dom_size, classes * 2 * share, modes), bf16),
            pltpu.VMEM((dom_size, classes * 2 * share, modes), bf16),
            pltpu.VMEM((classes, modes), f32),
            pltpu.VMEM((dom_size, classes, modes), f32),
            pltpu.VMEM((8, parts), f32),
            pltpu.VMEM((cls_size, 8, parts), f32),
            pltpu.VMEM((parts, cycles, angles), bf16),
            pltpu.VMEM(ctf_table.shape, f32),
            pltpu.VMEM((1, parts), jnp.int32),
            pltpu.VMEM((1, parts), jnp.int32),
            pltpu.VMEM((1, parts), f32),
            pltpu.VMEM((angles, angles), bf16),
            pltpu.VMEM((angles, angles), bf16),
            pltpu.VMEM((angles, angles), bf16),
            pltpu.VMEM((angles, angles), bf16),
            pltpu.SemaphoreType.DMA((16,)),
            pltpu.SemaphoreType.DMA((2, dom_size)),
            pltpu.SemaphoreType.DMA((2, cls_size)),
            pltpu.SemaphoreType.DMA((2, dom_size)),
            pltpu.SemaphoreType.DMA((2, dom_size)),
        ],
        compiler_params=pltpu.CompilerParams(
            collective_id=0, has_side_effects=True, vmem_limit_bytes=52 * 1024 * 1024
        ),
    )(
        images,
        class_refs.reshape(classes * share, angles),
        ctf_table,
        ctf_group[None, :],
        prior_angle[None, :],
        precision[None, :],
        *[jnp.asarray(table) for table in tables],
    )
    return new_refs.reshape(classes, share, angles), log_evidence.reshape(parts)


def pick(images, class_refs, *rest):
    parts, cycles, angles = images.shape
    classes, share, _ = class_refs.shape
    fits = angles == 256 and cycles == 64 and parts == 128 and share % 8 == 0 and classes % 16 == 0
    return (fused if fits else local)(images, class_refs, *rest)


def solution(mesh):
    in_specs = (P("dom", None, None), P("cls", "dom", None), P(), P("dom"), P("dom"), P("dom"))
    out_specs = (P("cls", "dom", None), P("dom"))
    return jax.shard_map(pick, mesh=mesh, in_specs=in_specs, out_specs=out_specs, check_vma=False)
```

```python
import functools
import math

import jax
import jax.numpy as jnp
import ml_dtypes
import numpy as np
from jax import lax
from jax.experimental import pallas as pl
from jax.experimental.pallas import tpu as pltpu
from jax.sharding import PartitionSpec as P

prior_strength = 2.0
ridge = 1.0
highest = lax.Precision.HIGHEST


def angle_table(angle_count, mode_count):
    angles = jnp.arange(angle_count, dtype=jnp.int32)
    freqs = jnp.arange(mode_count, dtype=jnp.int32)
    product = angles[:, None] * freqs[None, :] % angle_count
    phase = product.astype(jnp.float32) * (2.0 * math.pi / angle_count)
    return jnp.concatenate([jnp.cos(phase), jnp.sin(phase)], axis=1)


def split_table(forward):
    upper = forward.astype(jnp.bfloat16)
    lower = (forward - upper.astype(jnp.float32)).astype(jnp.bfloat16)
    return (upper, lower)


def mode_weights(angle_count, mode_count):
    freqs = jnp.arange(mode_count, dtype=jnp.int32)
    single = jnp.where(freqs == 0, 1.0, 2.0).astype(jnp.float32) / angle_count
    return jnp.concatenate([single, single])


def synthesis_table(angle_count, mode_count):
    return (
        jnp.transpose(angle_table(angle_count, mode_count))
        * mode_weights(angle_count, mode_count)[:, None]
    )


def spectrum(values, forward_pair):
    upper, lower = forward_pair
    flat = values.reshape(-1, values.shape[-1])
    result = jnp.dot(flat, upper, preferred_element_type=jnp.float32)
    result = result + jnp.dot(flat, lower, preferred_element_type=jnp.float32)
    return result.reshape(values.shape[:-1] + (upper.shape[1],))


def weighted_spectrum(images, ctf_rows, forward_pair):
    return (ctf_rows[:, :, None] * spectrum(images, forward_pair)).astype(jnp.bfloat16)


def prior_term(prior_angle, angle_count):
    rotations = jnp.arange(angle_count, dtype=jnp.int32)
    offsets = (rotations[None, :] - prior_angle[:, None]) % angle_count
    return prior_strength * jnp.cos(offsets.astype(jnp.float32) * (2.0 * math.pi / angle_count))


def pair_refs(spec_four):
    cos_part = spec_four[:, :, 0]
    sin_part = spec_four[:, :, 1]
    first_pair = jnp.stack([cos_part, sin_part], axis=2)
    second_pair = jnp.stack([-sin_part, cos_part], axis=2)
    return jnp.stack([first_pair, second_pair], axis=1)


def pair_weights(spec_four):
    cos_part = spec_four[:, :, 0]
    sin_part = spec_four[:, :, 1]
    first_pair = jnp.stack([cos_part, sin_part], axis=2)
    second_pair = jnp.stack([-sin_part, cos_part], axis=2)
    return jnp.stack([first_pair, second_pair], axis=2)


def local(images, class_refs, ctf_table, ctf_group, prior_angle, precision):
    particle_count, cycle_count, angle_count = images.shape
    mode_count = angle_count // 2
    class_count = class_refs.shape[0]
    forward = angle_table(angle_count, mode_count)
    forward_pair = split_table(forward)
    synthesis = synthesis_table(angle_count, mode_count)
    ref_local = spectrum(class_refs, forward_pair).astype(jnp.bfloat16)
    ref_spectra = lax.all_gather(ref_local, "dom", axis=1, tiled=True)
    group_ids = jnp.arange(ctf_table.shape[0], dtype=jnp.int32)
    one_hot = (ctf_group[:, None] == group_ids[None, :]).astype(jnp.float32)
    ctf_rows = jnp.dot(one_hot, ctf_table, precision=highest, preferred_element_type=jnp.float32)
    ctf_square = ctf_rows * ctf_rows
    particle_spectra = weighted_spectrum(images, ctf_rows, forward_pair)
    ref_float = ref_spectra.astype(jnp.float32)
    cycle_energy = jnp.sum(ref_float * ref_float * mode_weights(angle_count, mode_count), axis=2)
    energy = jnp.dot(
        ctf_square,
        jnp.transpose(cycle_energy),
        precision=highest,
        preferred_element_type=jnp.float32,
    )
    particle_four = particle_spectra.reshape(particle_count, cycle_count, 2, mode_count)
    ref_pairs = pair_refs(ref_spectra.reshape(class_count, cycle_count, 2, mode_count))
    cross = jnp.einsum(
        "prhm,kjrhm->pkjm", particle_four, ref_pairs, preferred_element_type=jnp.float32
    )
    correlation = jnp.dot(
        cross.reshape(-1, angle_count),
        synthesis,
        precision=highest,
        preferred_element_type=jnp.float32,
    )
    correlation = correlation.reshape(particle_count, class_count, angle_count)
    score = precision[:, None, None] * (correlation - 0.5 * energy[:, :, None])
    score = score + prior_term(prior_angle, angle_count)[:, None, :]
    row_top = jnp.max(score, axis=(1, 2))
    peak = lax.pmax(row_top, "cls")
    local_sum = jnp.sum(jnp.exp(score - peak[:, None, None]), axis=(1, 2))
    sum_exp = lax.psum(local_sum, "cls")
    log_evidence = peak + jnp.log(sum_exp)
    weights = jnp.exp(score - log_evidence[:, None, None]).astype(jnp.bfloat16)
    weight_spectra = spectrum(weights, forward_pair).astype(jnp.bfloat16)
    mass = jnp.sum(weights.astype(jnp.float32), axis=2)
    weight_pairs = pair_weights(weight_spectra.reshape(particle_count, class_count, 2, mode_count))
    class_sums = jnp.einsum(
        "pkjhm,prhm->rkjm", weight_pairs, particle_four, preferred_element_type=jnp.float32
    )
    class_sums = class_sums.reshape(cycle_count, class_count, angle_count)
    totals = jnp.dot(
        jnp.transpose(ctf_square), mass, precision=highest, preferred_element_type=jnp.float32
    )
    whole_sums, whole_totals = lax.psum((class_sums, totals), "dom")
    cycle_share = cycle_count // lax.axis_size("dom")
    cycle_start = lax.axis_index("dom") * cycle_share
    cycle_sums = lax.dynamic_slice_in_dim(whole_sums, cycle_start, cycle_share, 0)
    cycle_totals = lax.dynamic_slice_in_dim(whole_totals, cycle_start, cycle_share, 0)
    new_spectra = cycle_sums / (cycle_totals + ridge)[:, :, None]
    new_refs = jnp.dot(
        new_spectra.reshape(-1, angle_count),
        synthesis,
        precision=highest,
        preferred_element_type=jnp.float32,
    )
    new_refs = jnp.transpose(
        new_refs.reshape(cycle_sums.shape[0], class_count, angle_count), (1, 0, 2)
    )
    return (new_refs, log_evidence)


gap = 8


def block_at(index, size):
    return slice(index * (size + gap), index * (size + gap) + size)


def nt(left, right, precision=None):
    return lax.dot_general(
        left,
        right,
        (((1,), (1,)), ((), ())),
        precision=precision,
        preferred_element_type=jnp.float32,
    )


def nn(left, right, precision=None):
    return jnp.dot(left, right, precision=precision, preferred_element_type=jnp.float32)


def halves(value):
    upper = value.astype(jnp.bfloat16)
    lower = (value - upper.astype(jnp.float32)).astype(jnp.bfloat16)
    return upper, lower


def rounded(value):
    return value.astype(jnp.bfloat16).astype(jnp.float32)


def host_tables(angle_count, mode_count):
    product = np.outer(np.arange(angle_count), np.arange(mode_count)) % angle_count
    phase = product * (2.0 * math.pi / angle_count)
    forward = np.concatenate([np.cos(phase), np.sin(phase)], axis=1).astype(np.float32)
    single = np.where(np.arange(mode_count) == 0, 1.0, 2.0) / angle_count
    scale = np.concatenate([single, single]).astype(np.float32)
    inverse = forward * scale[None, :]

    def split(table):
        upper = table.astype(ml_dtypes.bfloat16)
        lower = (table - upper.astype(np.float32)).astype(ml_dtypes.bfloat16)
        return upper, lower

    return split(np.ascontiguousarray(forward.T)) + split(inverse)


def whole_kernel(
    dom_size, cls_size, img_in, refs_in, table_in, group_in, angle_in, prec_in, fwd_hi_in, fwd_lo_in, inv_hi_in, inv_lo_in,
    out_new, out_log, ref_slots, ref_rows, ctf, spec, ref_spec, cross, score, sums, send, recv,
    tot_send, tot_recv, stat_send, stat_recv, img, table, group, angle, prec, fwd_hi, fwd_lo, inv_hi, inv_lo, load_sems, ref_sems, stat_sems, sum_sems, tot_sems,
):
    mesh_ids = pl.DeviceIdType.MESH
    dom, cls = lax.axis_index("dom"), lax.axis_index("cls")
    parts, cycles, angles = img_in.shape
    modes = angles // 2
    share = cycles // dom_size
    classes = refs_in.shape[0] // share
    barrier = pltpu.get_barrier_semaphore()
    for step in range(1, dom_size):
        pl.semaphore_signal(barrier, inc=1, device_id={"dom": lax.rem(dom + step, dom_size)}, device_id_type=mesh_ids)
    for step in range(1, cls_size):
        pl.semaphore_signal(barrier, inc=1, device_id={"cls": lax.rem(cls + step, cls_size)}, device_id_type=mesh_ids)

    early = parts // 16
    pieces = [pl.ds(start, early * 4) for start in range(0, parts, early * 4)]
    small = [
        (table_in, table), (group_in, group), (fwd_hi_in, fwd_hi), (fwd_lo_in, fwd_lo),
        (img_in.at[pieces[0]], img.at[pieces[0]]),
    ]
    late = [(img_in.at[piece], img.at[piece]) for piece in pieces[1:]] + [
        (angle_in, angle), (prec_in, prec), (inv_hi_in, inv_hi), (inv_lo_in, inv_lo), (refs_in, ref_slots.at[0])
    ]
    loads = [
        pltpu.make_async_copy(source, target, load_sems.at[place])
        for place, (source, target) in enumerate(small + late)
    ]
    for load in loads:
        load.start()

    def remote(source, target, sems, axis, place, size, step):
        return pltpu.make_async_remote_copy(
            src_ref=source,
            dst_ref=target,
            send_sem=sems.at[0, step],
            recv_sem=sems.at[1, step],
            device_id={axis: lax.rem(place + step, size)},
            device_id_type=mesh_ids,
        )

    ref_copies = [
        remote(refs_in, ref_slots.at[step], ref_sems, "dom", dom, dom_size, step)
        for step in range(1, dom_size)
    ]
    lanes = lax.broadcasted_iota(jnp.int32, (modes, modes), 1)
    low = lanes < cycles
    for load in loads[: len(small)]:
        load.wait()
    groups = lax.broadcasted_iota(jnp.int32, (table.shape[0], parts), 0)
    one_hot = (groups == group[...]).astype(jnp.float32)
    doubled = jnp.concatenate([table[...], table[...]], axis=1)
    ctf[...] = lax.dot_general(
        one_hot, doubled, (((0,), (0,)), ((), ())), precision=highest, preferred_element_type=jnp.float32
    )

    def transform(block):
        result = nt(fwd_hi[...], block) + nt(fwd_lo[...], block)
        found = []
        for pair in range(2):
            top = result[:modes, pair * modes : (pair + 1) * modes]
            bottom = result[modes:, pair * modes : (pair + 1) * modes]
            found.append(jnp.where(low, top, pltpu.roll(bottom, cycles, 1)))
            found.append(jnp.where(low, pltpu.roll(top, cycles, 1), bottom))
        return found

    def image_step(step, carry):
        first = step * 4
        block = img[pl.ds(first, 4)].reshape(4 * cycles, angles)
        for offset, value in enumerate(transform(block)):
            row = ctf[pl.ds(first + offset, 1), :]
            spec[pl.ds(first + offset, modes, stride=parts + gap), :] = value * row
        return carry

    lax.fori_loop(0, early, image_step, 0, unroll=4)
    pl.semaphore_wait(barrier, dom_size + cls_size - 2)
    for copy in ref_copies:
        copy.start()
    for load in loads[len(small) :]:
        load.wait()
    lax.fori_loop(early, parts // 4, image_step, 0, unroll=4)

    turns = lax.broadcasted_iota(jnp.int32, (angles, parts), 0)
    offsets = (turns - angle[...] + angles) % angles
    prior = prior_strength * jnp.cos(offsets.astype(jnp.float32) * (2.0 * math.pi / angles))

    for copy in ref_copies:
        copy.wait()
    for step in range(dom_size):
        source = ref_slots[step].astype(jnp.float32).reshape(classes, share, angles)
        owner = lax.rem(dom - step + dom_size, dom_size)
        ref_rows[:, pl.ds(pl.multiple_of(owner * share, share), share), :] = source
    rows = lax.broadcasted_iota(jnp.int32, (modes, modes), 0)
    weight = jnp.where(rows == 0, 1.0, 2.0) * (1.0 / angles)
    sign = jnp.where(lax.broadcasted_iota(jnp.int32, (classes, modes), 1) < cycles, 1.0, -1.0)
    energies = []
    for step in range(classes // 4):
        block = ref_rows[step * 4 : step * 4 + 4].reshape(4 * cycles, angles).astype(jnp.bfloat16)
        for offset, value in enumerate(transform(block)):
            index = step * 4 + offset
            value = rounded(value)
            energies.append(jnp.sum(value * value * weight, axis=0, keepdims=True))
            ref_spec[pl.ds(index, modes, stride=2 * classes + gap), :] = value
            turned = pltpu.roll(value, cycles, 1)
            ref_spec[pl.ds(classes + index, modes, stride=2 * classes + gap), :] = jnp.where(low, -turned, turned)
    ctf_square = ctf[...] * ctf[...]
    energy = nt(jnp.concatenate(energies, axis=0), ctf_square, highest)

    def cross_step(mode, carry):
        particles = spec[pl.ds(pl.multiple_of(mode * (parts + gap), gap), parts), :].astype(jnp.bfloat16)
        others = ref_spec[pl.ds(pl.multiple_of(mode * (2 * classes + gap), gap), 2 * classes), :]
        cross[pl.ds(mode, 2 * classes, stride=modes + gap), :] = nt(others.astype(jnp.bfloat16), particles)
        return carry

    lax.fori_loop(0, modes, cross_step, 0, unroll=64)

    scale = prec[...]
    peak = None
    for index in range(classes):
        both = jnp.concatenate(
            [cross[block_at(index, modes), :],
             cross[block_at(classes + index, modes), :]], axis=0)
        upper, lower = halves(both)
        found = nn(inv_hi[...], upper) + (nn(inv_hi[...], lower) + nn(inv_lo[...], upper))
        found = scale * (found - 0.5 * energy[index : index + 1, :]) + prior
        score[index] = found
        top = jnp.max(found, axis=0, keepdims=True)
        peak = top if peak is None else jnp.maximum(peak, top)
    total = jnp.zeros((1, parts), jnp.float32)
    for index in range(classes):
        total = total + jnp.sum(jnp.exp(score[index] - peak), axis=0, keepdims=True)
    stat_send[...] = jnp.concatenate([peak] * 4 + [total] * 4, axis=0)
    stat_copies = [
        remote(stat_send, stat_recv.at[step], stat_sems, "cls", cls, cls_size, step)
        for step in range(1, cls_size)
    ]
    for copy in stat_copies:
        copy.start()
    for copy in stat_copies:
        copy.wait()
    pairs = [(peak, total)]
    for step in range(1, cls_size):
        pairs.append((stat_recv[step, 0:1, :], stat_recv[step, 4:5, :]))
    best = peak
    for other, _ in pairs[1:]:
        best = jnp.maximum(best, other)
    whole = jnp.zeros((1, parts), jnp.float32)
    for other, part in pairs:
        whole = whole + part * jnp.exp(other - best)
    log_evidence = best + jnp.log(whole)
    out_log[...] = log_evidence

    masses = []
    for index in range(classes):
        weights = jnp.exp(score[index] - log_evidence).astype(jnp.bfloat16)
        masses.append(jnp.sum(weights.astype(jnp.float32), axis=0, keepdims=True))
        found = nn(fwd_hi[...], weights) + nn(fwd_lo[...], weights)
        cross[block_at(index, modes), :] = found[:modes]
        cross[block_at(classes + index, modes), :] = found[modes:]
    tot_send[...] = nn(jnp.concatenate(masses, axis=0), ctf_square, highest)
    tot_copies = [
        remote(tot_send, tot_recv.at[step], tot_sems, "dom", dom, dom_size, step)
        for step in range(1, dom_size)
    ]
    for copy in tot_copies:
        copy.start()

    def sum_step(mode, carry):
        particles = spec[pl.ds(pl.multiple_of(mode * (parts + gap), gap), parts), :].astype(jnp.bfloat16)
        weights = cross[pl.ds(mode, 2 * classes, stride=modes + gap), :].astype(jnp.bfloat16)
        found = nn(weights, particles)
        found = found[:classes] + sign * pltpu.roll(found[classes:], cycles, 1)
        sums[pl.ds(mode, classes, stride=modes + gap), :] = found
        return carry

    lax.fori_loop(0, modes, sum_step, 0, unroll=64)

    for index in range(classes):
        turned = jnp.transpose(sums[block_at(index, modes), :])
        for part in range(dom_size):
            piece = jnp.concatenate(
                [turned[part * share : (part + 1) * share],
                 turned[cycles + part * share : cycles + (part + 1) * share]], axis=0)
            send[part, index * 2 * share : (index + 1) * 2 * share, :] = piece.astype(jnp.bfloat16)
    sum_copies = [
        remote(send.at[lax.rem(dom + step, dom_size)], recv.at[step], sum_sems, "dom", dom, dom_size, step)
        for step in range(1, dom_size)
    ]
    for copy in sum_copies:
        copy.start()
    for copy in tot_copies:
        copy.wait()
    totals = tot_send[...]
    for step in range(1, dom_size):
        totals = totals + tot_recv[step]
    columns = lax.broadcasted_iota(jnp.int32, (1, share, modes), 2)
    wanted = lax.broadcasted_iota(jnp.int32, (1, share, modes), 1) + dom * share
    picked = jnp.where(columns == wanted, totals[:, None, :], 0.0)
    divisor = jnp.sum(picked, axis=2, keepdims=True).reshape(classes * share, 1) + ridge
    for copy in sum_copies:
        copy.wait()
    gathered = send[dom].astype(jnp.float32)
    for step in range(1, dom_size):
        gathered = gathered + recv[step].astype(jnp.float32)
    gathered = gathered.reshape(classes, 2, share, modes)
    result = jnp.zeros((classes * share, angles), jnp.float32)
    for half in range(2):
        upper, lower = halves(gathered[:, half].reshape(classes * share, modes))
        hi = inv_hi[:, half * modes : (half + 1) * modes]
        lo = inv_lo[:, half * modes : (half + 1) * modes]
        result = result + nt(upper, hi) + (nt(lower, hi) + nt(upper, lo))
    out_new[...] = result / divisor


def fused(images, class_refs, ctf_table, ctf_group, prior_angle, precision):
    dom_size, cls_size = lax.axis_size("dom"), lax.axis_size("cls")
    parts, cycles, angles = images.shape
    modes = angles // 2
    classes, share, _ = class_refs.shape
    tables = host_tables(angles, modes)
    f32, bf16 = jnp.float32, jnp.bfloat16
    vmem = pl.BlockSpec(memory_space=pltpu.VMEM)
    new_refs, log_evidence = pl.pallas_call(
        functools.partial(whole_kernel, dom_size, cls_size),
        out_shape=(
            jax.ShapeDtypeStruct((classes * share, angles), f32),
            jax.ShapeDtypeStruct((1, parts), f32),
        ),
        in_specs=[pl.BlockSpec(memory_space=pltpu.HBM)] * 10,
        out_specs=(vmem, vmem),
        scratch_shapes=[
            pltpu.VMEM((dom_size, classes * share, angles), bf16),
            pltpu.VMEM((classes, cycles, angles), f32),
            pltpu.VMEM((parts, modes), f32),
            pltpu.VMEM((modes * (parts + gap), modes), f32),
            pltpu.VMEM((modes * (2 * classes + gap), modes), f32),
            pltpu.VMEM((2 * classes * (modes + gap), parts), f32),
            pltpu.VMEM((classes, angles, parts), f32),
            pltpu.VMEM((classes * (modes + gap), modes), f32),
            pltpu.VMEM((dom_size, classes * 2 * share, modes), bf16),
            pltpu.VMEM((dom_size, classes * 2 * share, modes), bf16),
            pltpu.VMEM((classes, modes), f32),
            pltpu.VMEM((dom_size, classes, modes), f32),
            pltpu.VMEM((8, parts), f32),
            pltpu.VMEM((cls_size, 8, parts), f32),
            pltpu.VMEM((parts, cycles, angles), bf16),
            pltpu.VMEM(ctf_table.shape, f32),
            pltpu.VMEM((1, parts), jnp.int32),
            pltpu.VMEM((1, parts), jnp.int32),
            pltpu.VMEM((1, parts), f32),
            pltpu.VMEM((angles, angles), bf16),
            pltpu.VMEM((angles, angles), bf16),
            pltpu.VMEM((angles, angles), bf16),
            pltpu.VMEM((angles, angles), bf16),
            pltpu.SemaphoreType.DMA((16,)),
            pltpu.SemaphoreType.DMA((2, dom_size)),
            pltpu.SemaphoreType.DMA((2, cls_size)),
            pltpu.SemaphoreType.DMA((2, dom_size)),
            pltpu.SemaphoreType.DMA((2, dom_size)),
        ],
        compiler_params=pltpu.CompilerParams(
            collective_id=0, has_side_effects=True, vmem_limit_bytes=63 * 1024 * 1024
        ),
    )(
        images,
        class_refs.reshape(classes * share, angles),
        ctf_table,
        ctf_group[None, :],
        prior_angle[None, :],
        precision[None, :],
        *[jnp.asarray(table) for table in tables],
    )
    return new_refs.reshape(classes, share, angles), log_evidence.reshape(parts)


def pick(images, class_refs, *rest):
    parts, cycles, angles = images.shape
    classes, share, _ = class_refs.shape
    fits = angles == 256 and cycles == 64 and parts == 128 and share % 8 == 0 and classes % 16 == 0
    return (fused if fits else local)(images, class_refs, *rest)


def solution(mesh):
    in_specs = (P("dom", None, None), P("cls", "dom", None), P(), P("dom"), P("dom"), P("dom"))
    out_specs = (P("cls", "dom", None), P("dom"))
    return jax.shard_map(pick, mesh=mesh, in_specs=in_specs, out_specs=out_specs, check_vma=False)
```

```python
import functools
import math

import jax
import jax.numpy as jnp
import ml_dtypes
import numpy as np
from jax import lax
from jax.experimental import pallas as pl
from jax.experimental.pallas import tpu as pltpu
from jax.sharding import PartitionSpec as P

prior_strength = 2.0
ridge = 1.0
highest = lax.Precision.HIGHEST


def angle_table(angle_count, mode_count):
    angles = jnp.arange(angle_count, dtype=jnp.int32)
    freqs = jnp.arange(mode_count, dtype=jnp.int32)
    product = angles[:, None] * freqs[None, :] % angle_count
    phase = product.astype(jnp.float32) * (2.0 * math.pi / angle_count)
    return jnp.concatenate([jnp.cos(phase), jnp.sin(phase)], axis=1)


def split_table(forward):
    upper = forward.astype(jnp.bfloat16)
    lower = (forward - upper.astype(jnp.float32)).astype(jnp.bfloat16)
    return (upper, lower)


def mode_weights(angle_count, mode_count):
    freqs = jnp.arange(mode_count, dtype=jnp.int32)
    single = jnp.where(freqs == 0, 1.0, 2.0).astype(jnp.float32) / angle_count
    return jnp.concatenate([single, single])


def synthesis_table(angle_count, mode_count):
    return (
        jnp.transpose(angle_table(angle_count, mode_count))
        * mode_weights(angle_count, mode_count)[:, None]
    )


def spectrum(values, forward_pair):
    upper, lower = forward_pair
    flat = values.reshape(-1, values.shape[-1])
    result = jnp.dot(flat, upper, preferred_element_type=jnp.float32)
    result = result + jnp.dot(flat, lower, preferred_element_type=jnp.float32)
    return result.reshape(values.shape[:-1] + (upper.shape[1],))


def weighted_spectrum(images, ctf_rows, forward_pair):
    return (ctf_rows[:, :, None] * spectrum(images, forward_pair)).astype(jnp.bfloat16)


def prior_term(prior_angle, angle_count):
    rotations = jnp.arange(angle_count, dtype=jnp.int32)
    offsets = (rotations[None, :] - prior_angle[:, None]) % angle_count
    return prior_strength * jnp.cos(offsets.astype(jnp.float32) * (2.0 * math.pi / angle_count))


def pair_refs(spec_four):
    cos_part = spec_four[:, :, 0]
    sin_part = spec_four[:, :, 1]
    first_pair = jnp.stack([cos_part, sin_part], axis=2)
    second_pair = jnp.stack([-sin_part, cos_part], axis=2)
    return jnp.stack([first_pair, second_pair], axis=1)


def pair_weights(spec_four):
    cos_part = spec_four[:, :, 0]
    sin_part = spec_four[:, :, 1]
    first_pair = jnp.stack([cos_part, sin_part], axis=2)
    second_pair = jnp.stack([-sin_part, cos_part], axis=2)
    return jnp.stack([first_pair, second_pair], axis=2)


def local(images, class_refs, ctf_table, ctf_group, prior_angle, precision):
    particle_count, cycle_count, angle_count = images.shape
    mode_count = angle_count // 2
    class_count = class_refs.shape[0]
    forward = angle_table(angle_count, mode_count)
    forward_pair = split_table(forward)
    synthesis = synthesis_table(angle_count, mode_count)
    ref_local = spectrum(class_refs, forward_pair).astype(jnp.bfloat16)
    ref_spectra = lax.all_gather(ref_local, "dom", axis=1, tiled=True)
    group_ids = jnp.arange(ctf_table.shape[0], dtype=jnp.int32)
    one_hot = (ctf_group[:, None] == group_ids[None, :]).astype(jnp.float32)
    ctf_rows = jnp.dot(one_hot, ctf_table, precision=highest, preferred_element_type=jnp.float32)
    ctf_square = ctf_rows * ctf_rows
    particle_spectra = weighted_spectrum(images, ctf_rows, forward_pair)
    ref_float = ref_spectra.astype(jnp.float32)
    cycle_energy = jnp.sum(ref_float * ref_float * mode_weights(angle_count, mode_count), axis=2)
    energy = jnp.dot(
        ctf_square,
        jnp.transpose(cycle_energy),
        precision=highest,
        preferred_element_type=jnp.float32,
    )
    particle_four = particle_spectra.reshape(particle_count, cycle_count, 2, mode_count)
    ref_pairs = pair_refs(ref_spectra.reshape(class_count, cycle_count, 2, mode_count))
    cross = jnp.einsum(
        "prhm,kjrhm->pkjm", particle_four, ref_pairs, preferred_element_type=jnp.float32
    )
    correlation = jnp.dot(
        cross.reshape(-1, angle_count),
        synthesis,
        precision=highest,
        preferred_element_type=jnp.float32,
    )
    correlation = correlation.reshape(particle_count, class_count, angle_count)
    score = precision[:, None, None] * (correlation - 0.5 * energy[:, :, None])
    score = score + prior_term(prior_angle, angle_count)[:, None, :]
    row_top = jnp.max(score, axis=(1, 2))
    peak = lax.pmax(row_top, "cls")
    local_sum = jnp.sum(jnp.exp(score - peak[:, None, None]), axis=(1, 2))
    sum_exp = lax.psum(local_sum, "cls")
    log_evidence = peak + jnp.log(sum_exp)
    weights = jnp.exp(score - log_evidence[:, None, None]).astype(jnp.bfloat16)
    weight_spectra = spectrum(weights, forward_pair).astype(jnp.bfloat16)
    mass = jnp.sum(weights.astype(jnp.float32), axis=2)
    weight_pairs = pair_weights(weight_spectra.reshape(particle_count, class_count, 2, mode_count))
    class_sums = jnp.einsum(
        "pkjhm,prhm->rkjm", weight_pairs, particle_four, preferred_element_type=jnp.float32
    )
    class_sums = class_sums.reshape(cycle_count, class_count, angle_count)
    totals = jnp.dot(
        jnp.transpose(ctf_square), mass, precision=highest, preferred_element_type=jnp.float32
    )
    whole_sums, whole_totals = lax.psum((class_sums, totals), "dom")
    cycle_share = cycle_count // lax.axis_size("dom")
    cycle_start = lax.axis_index("dom") * cycle_share
    cycle_sums = lax.dynamic_slice_in_dim(whole_sums, cycle_start, cycle_share, 0)
    cycle_totals = lax.dynamic_slice_in_dim(whole_totals, cycle_start, cycle_share, 0)
    new_spectra = cycle_sums / (cycle_totals + ridge)[:, :, None]
    new_refs = jnp.dot(
        new_spectra.reshape(-1, angle_count),
        synthesis,
        precision=highest,
        preferred_element_type=jnp.float32,
    )
    new_refs = jnp.transpose(
        new_refs.reshape(cycle_sums.shape[0], class_count, angle_count), (1, 0, 2)
    )
    return (new_refs, log_evidence)


gap = 8


def block_at(index, size):
    return slice(index * (size + gap), index * (size + gap) + size)


def nt(left, right, precision=None):
    return lax.dot_general(
        left,
        right,
        (((1,), (1,)), ((), ())),
        precision=precision,
        preferred_element_type=jnp.float32,
    )


def nn(left, right, precision=None):
    return jnp.dot(left, right, precision=precision, preferred_element_type=jnp.float32)


def halves(value):
    upper = value.astype(jnp.bfloat16)
    lower = (value - upper.astype(jnp.float32)).astype(jnp.bfloat16)
    return upper, lower


def rounded(value):
    return value.astype(jnp.bfloat16).astype(jnp.float32)


def host_tables(angle_count, mode_count):
    product = np.outer(np.arange(angle_count), np.arange(mode_count)) % angle_count
    phase = product * (2.0 * math.pi / angle_count)
    forward = np.concatenate([np.cos(phase), np.sin(phase)], axis=1).astype(np.float32)
    single = np.where(np.arange(mode_count) == 0, 1.0, 2.0) / angle_count
    scale = np.concatenate([single, single]).astype(np.float32)
    inverse = forward * scale[None, :]

    def split(table):
        upper = table.astype(ml_dtypes.bfloat16)
        lower = (table - upper.astype(np.float32)).astype(ml_dtypes.bfloat16)
        return upper, lower

    return split(np.ascontiguousarray(forward.T)) + split(inverse)


def whole_kernel(
    dom_size, cls_size, img_in, refs_in, table_in, group_in, angle_in, prec_in, fwd_hi_in, fwd_lo_in, inv_hi_in, inv_lo_in,
    out_new, out_log, ref_slots, ref_rows, ctf, spec, ref_spec, cross, score, sums, send, recv,
    tot_send, tot_recv, stat_send, stat_recv, img, table, group, angle, prec, fwd_hi, fwd_lo, inv_hi, inv_lo, load_sems, ref_sems, stat_sems, sum_sems, tot_sems,
):
    mesh_ids = pl.DeviceIdType.MESH
    dom, cls = lax.axis_index("dom"), lax.axis_index("cls")
    parts, cycles, angles = img_in.shape
    modes = angles // 2
    share = cycles // dom_size
    classes = refs_in.shape[0] // share
    barrier = pltpu.get_barrier_semaphore()
    for step in range(1, dom_size):
        pl.semaphore_signal(barrier, inc=1, device_id={"dom": lax.rem(dom + step, dom_size)}, device_id_type=mesh_ids)
    for step in range(1, cls_size):
        pl.semaphore_signal(barrier, inc=1, device_id={"cls": lax.rem(cls + step, cls_size)}, device_id_type=mesh_ids)

    early = parts // 16
    pieces = [pl.ds(start, early * 4) for start in range(0, parts, early * 4)]
    small = [
        (table_in, table), (group_in, group), (fwd_hi_in, fwd_hi), (fwd_lo_in, fwd_lo),
        (img_in.at[pieces[0]], img.at[pieces[0]]),
    ]
    late = [(img_in.at[piece], img.at[piece]) for piece in pieces[1:]] + [
        (angle_in, angle), (prec_in, prec), (inv_hi_in, inv_hi), (inv_lo_in, inv_lo), (refs_in, ref_slots.at[0])
    ]
    loads = [
        pltpu.make_async_copy(source, target, load_sems.at[place])
        for place, (source, target) in enumerate(small + late)
    ]
    for load in loads:
        load.start()

    def remote(source, target, sems, axis, place, size, step):
        return pltpu.make_async_remote_copy(
            src_ref=source,
            dst_ref=target,
            send_sem=sems.at[0, step],
            recv_sem=sems.at[1, step],
            device_id={axis: lax.rem(place + step, size)},
            device_id_type=mesh_ids,
        )

    ref_copies = [
        remote(refs_in, ref_slots.at[step], ref_sems, "dom", dom, dom_size, step)
        for step in range(1, dom_size)
    ]
    lanes = lax.broadcasted_iota(jnp.int32, (modes, modes), 1)
    low = lanes < cycles
    for load in loads[: len(small)]:
        load.wait()
    groups = lax.broadcasted_iota(jnp.int32, (table.shape[0], parts), 0)
    one_hot = (groups == group[...]).astype(jnp.float32)
    doubled = jnp.concatenate([table[...], table[...]], axis=1)
    ctf[...] = lax.dot_general(
        one_hot, doubled, (((0,), (0,)), ((), ())), precision=highest, preferred_element_type=jnp.float32
    )

    def transform(block):
        result = nt(fwd_hi[...], block) + nt(fwd_lo[...], block)
        found = []
        for pair in range(2):
            top = result[:modes, pair * modes : (pair + 1) * modes]
            bottom = result[modes:, pair * modes : (pair + 1) * modes]
            found.append(jnp.where(low, top, pltpu.roll(bottom, cycles, 1)))
            found.append(jnp.where(low, pltpu.roll(top, cycles, 1), bottom))
        return found

    def image_step(step, carry):
        first = step * 4
        block = img[pl.ds(first, 4)].reshape(4 * cycles, angles)
        for offset, value in enumerate(transform(block)):
            row = ctf[pl.ds(first + offset, 1), :]
            spec[pl.ds(first + offset, modes, stride=parts + gap), :] = value * row
        return carry

    lax.fori_loop(0, early, image_step, 0, unroll=8)
    pl.semaphore_wait(barrier, dom_size + cls_size - 2)
    for copy in ref_copies:
        copy.start()
    for load in loads[len(small) :]:
        load.wait()
    lax.fori_loop(early, parts // 4, image_step, 0, unroll=8)

    turns = lax.broadcasted_iota(jnp.int32, (angles, parts), 0)
    offsets = (turns - angle[...] + angles) % angles
    prior = prior_strength * jnp.cos(offsets.astype(jnp.float32) * (2.0 * math.pi / angles))

    for copy in ref_copies:
        copy.wait()
    for step in range(dom_size):
        source = ref_slots[step].astype(jnp.float32).reshape(classes, share, angles)
        owner = lax.rem(dom - step + dom_size, dom_size)
        ref_rows[:, pl.ds(pl.multiple_of(owner * share, share), share), :] = source
    rows = lax.broadcasted_iota(jnp.int32, (modes, modes), 0)
    weight = jnp.where(rows == 0, 1.0, 2.0) * (1.0 / angles)
    sign = jnp.where(lax.broadcasted_iota(jnp.int32, (classes, modes), 1) < cycles, 1.0, -1.0)
    energies = []
    for step in range(classes // 4):
        block = ref_rows[step * 4 : step * 4 + 4].reshape(4 * cycles, angles).astype(jnp.bfloat16)
        for offset, value in enumerate(transform(block)):
            index = step * 4 + offset
            value = rounded(value)
            energies.append(jnp.sum(value * value * weight, axis=0, keepdims=True))
            ref_spec[pl.ds(index, modes, stride=2 * classes + gap), :] = value
            turned = pltpu.roll(value, cycles, 1)
            ref_spec[pl.ds(classes + index, modes, stride=2 * classes + gap), :] = jnp.where(low, -turned, turned)
    ctf_square = ctf[...] * ctf[...]
    energy = nt(jnp.concatenate(energies, axis=0), ctf_square, highest)

    def cross_step(mode, carry):
        particles = spec[pl.ds(pl.multiple_of(mode * (parts + gap), gap), parts), :].astype(jnp.bfloat16)
        others = ref_spec[pl.ds(pl.multiple_of(mode * (2 * classes + gap), gap), 2 * classes), :]
        cross[pl.ds(mode, 2 * classes, stride=modes + gap), :] = nt(others.astype(jnp.bfloat16), particles)
        return carry

    lax.fori_loop(0, modes, cross_step, 0, unroll=128)

    scale = prec[...]
    peak = None
    for index in range(classes):
        both = jnp.concatenate(
            [cross[block_at(index, modes), :],
             cross[block_at(classes + index, modes), :]], axis=0)
        upper, lower = halves(both)
        found = nn(inv_hi[...], upper) + (nn(inv_hi[...], lower) + nn(inv_lo[...], upper))
        found = scale * (found - 0.5 * energy[index : index + 1, :]) + prior
        score[index] = found
        top = jnp.max(found, axis=0, keepdims=True)
        peak = top if peak is None else jnp.maximum(peak, top)
    total = jnp.zeros((1, parts), jnp.float32)
    for index in range(classes):
        total = total + jnp.sum(jnp.exp(score[index] - peak), axis=0, keepdims=True)
    stat_send[...] = jnp.concatenate([peak] * 4 + [total] * 4, axis=0)
    stat_copies = [
        remote(stat_send, stat_recv.at[step], stat_sems, "cls", cls, cls_size, step)
        for step in range(1, cls_size)
    ]
    for copy in stat_copies:
        copy.start()
    for copy in stat_copies:
        copy.wait()
    pairs = [(peak, total)]
    for step in range(1, cls_size):
        pairs.append((stat_recv[step, 0:1, :], stat_recv[step, 4:5, :]))
    best = peak
    for other, _ in pairs[1:]:
        best = jnp.maximum(best, other)
    whole = jnp.zeros((1, parts), jnp.float32)
    for other, part in pairs:
        whole = whole + part * jnp.exp(other - best)
    log_evidence = best + jnp.log(whole)
    out_log[...] = log_evidence

    masses = []
    for index in range(classes):
        weights = jnp.exp(score[index] - log_evidence).astype(jnp.bfloat16)
        masses.append(jnp.sum(weights.astype(jnp.float32), axis=0, keepdims=True))
        found = nn(fwd_hi[...], weights) + nn(fwd_lo[...], weights)
        cross[block_at(index, modes), :] = found[:modes]
        cross[block_at(classes + index, modes), :] = found[modes:]
    tot_send[...] = nn(jnp.concatenate(masses, axis=0), ctf_square, highest)
    tot_copies = [
        remote(tot_send, tot_recv.at[step], tot_sems, "dom", dom, dom_size, step)
        for step in range(1, dom_size)
    ]
    for copy in tot_copies:
        copy.start()

    def sum_step(mode, carry):
        particles = spec[pl.ds(pl.multiple_of(mode * (parts + gap), gap), parts), :].astype(jnp.bfloat16)
        weights = cross[pl.ds(mode, 2 * classes, stride=modes + gap), :].astype(jnp.bfloat16)
        found = nn(weights, particles)
        found = found[:classes] + sign * pltpu.roll(found[classes:], cycles, 1)
        sums[pl.ds(mode, classes, stride=modes + gap), :] = found
        return carry

    lax.fori_loop(0, modes, sum_step, 0, unroll=128)

    for index in range(classes):
        turned = jnp.transpose(sums[block_at(index, modes), :])
        for part in range(dom_size):
            piece = jnp.concatenate(
                [turned[part * share : (part + 1) * share],
                 turned[cycles + part * share : cycles + (part + 1) * share]], axis=0)
            send[part, index * 2 * share : (index + 1) * 2 * share, :] = piece.astype(jnp.bfloat16)
    sum_copies = [
        remote(send.at[lax.rem(dom + step, dom_size)], recv.at[step], sum_sems, "dom", dom, dom_size, step)
        for step in range(1, dom_size)
    ]
    for copy in sum_copies:
        copy.start()
    for copy in tot_copies:
        copy.wait()
    totals = tot_send[...]
    for step in range(1, dom_size):
        totals = totals + tot_recv[step]
    columns = lax.broadcasted_iota(jnp.int32, (1, share, modes), 2)
    wanted = lax.broadcasted_iota(jnp.int32, (1, share, modes), 1) + dom * share
    picked = jnp.where(columns == wanted, totals[:, None, :], 0.0)
    divisor = jnp.sum(picked, axis=2, keepdims=True).reshape(classes * share, 1) + ridge
    for copy in sum_copies:
        copy.wait()
    gathered = send[dom].astype(jnp.float32)
    for step in range(1, dom_size):
        gathered = gathered + recv[step].astype(jnp.float32)
    gathered = gathered.reshape(classes, 2, share, modes)
    result = jnp.zeros((classes * share, angles), jnp.float32)
    for half in range(2):
        upper, lower = halves(gathered[:, half].reshape(classes * share, modes))
        hi = inv_hi[:, half * modes : (half + 1) * modes]
        lo = inv_lo[:, half * modes : (half + 1) * modes]
        result = result + nt(upper, hi) + (nt(lower, hi) + nt(upper, lo))
    out_new[...] = result / divisor


def fused(images, class_refs, ctf_table, ctf_group, prior_angle, precision):
    dom_size, cls_size = lax.axis_size("dom"), lax.axis_size("cls")
    parts, cycles, angles = images.shape
    modes = angles // 2
    classes, share, _ = class_refs.shape
    tables = host_tables(angles, modes)
    f32, bf16 = jnp.float32, jnp.bfloat16
    vmem = pl.BlockSpec(memory_space=pltpu.VMEM)
    new_refs, log_evidence = pl.pallas_call(
        functools.partial(whole_kernel, dom_size, cls_size),
        out_shape=(
            jax.ShapeDtypeStruct((classes * share, angles), f32),
            jax.ShapeDtypeStruct((1, parts), f32),
        ),
        in_specs=[pl.BlockSpec(memory_space=pltpu.HBM)] * 10,
        out_specs=(vmem, vmem),
        scratch_shapes=[
            pltpu.VMEM((dom_size, classes * share, angles), bf16),
            pltpu.VMEM((classes, cycles, angles), f32),
            pltpu.VMEM((parts, modes), f32),
            pltpu.VMEM((modes * (parts + gap), modes), f32),
            pltpu.VMEM((modes * (2 * classes + gap), modes), f32),
            pltpu.VMEM((2 * classes * (modes + gap), parts), f32),
            pltpu.VMEM((classes, angles, parts), f32),
            pltpu.VMEM((classes * (modes + gap), modes), f32),
            pltpu.VMEM((dom_size, classes * 2 * share, modes), bf16),
            pltpu.VMEM((dom_size, classes * 2 * share, modes), bf16),
            pltpu.VMEM((classes, modes), f32),
            pltpu.VMEM((dom_size, classes, modes), f32),
            pltpu.VMEM((8, parts), f32),
            pltpu.VMEM((cls_size, 8, parts), f32),
            pltpu.VMEM((parts, cycles, angles), bf16),
            pltpu.VMEM(ctf_table.shape, f32),
            pltpu.VMEM((1, parts), jnp.int32),
            pltpu.VMEM((1, parts), jnp.int32),
            pltpu.VMEM((1, parts), f32),
            pltpu.VMEM((angles, angles), bf16),
            pltpu.VMEM((angles, angles), bf16),
            pltpu.VMEM((angles, angles), bf16),
            pltpu.VMEM((angles, angles), bf16),
            pltpu.SemaphoreType.DMA((16,)),
            pltpu.SemaphoreType.DMA((2, dom_size)),
            pltpu.SemaphoreType.DMA((2, cls_size)),
            pltpu.SemaphoreType.DMA((2, dom_size)),
            pltpu.SemaphoreType.DMA((2, dom_size)),
        ],
        compiler_params=pltpu.CompilerParams(
            collective_id=0, has_side_effects=True, vmem_limit_bytes=63 * 1024 * 1024
        ),
    )(
        images,
        class_refs.reshape(classes * share, angles),
        ctf_table,
        ctf_group[None, :],
        prior_angle[None, :],
        precision[None, :],
        *[jnp.asarray(table) for table in tables],
    )
    return new_refs.reshape(classes, share, angles), log_evidence.reshape(parts)


def pick(images, class_refs, *rest):
    parts, cycles, angles = images.shape
    classes, share, _ = class_refs.shape
    fits = angles == 256 and cycles == 64 and parts == 128 and share % 8 == 0 and classes % 16 == 0
    return (fused if fits else local)(images, class_refs, *rest)


def solution(mesh):
    in_specs = (P("dom", None, None), P("cls", "dom", None), P(), P("dom"), P("dom"), P("dom"))
    out_specs = (P("cls", "dom", None), P("dom"))
    return jax.shard_map(pick, mesh=mesh, in_specs=in_specs, out_specs=out_specs, check_vma=False)
```
